512 devices in a mesh: enc: 64 (over y, x, core), mdl: 8 (over z).
Axes of the slice: x: 4, y: 8, z: 8, core: 2. Of those that a mesh axis runs over, the one named last changes fastest.
Arguments:
- tile_feats: bfloat16 [256, 8, 8, 1536], P('enc'), may hold values from -6 to 6
- dw_weight: bfloat16 [7, 7, 1536], replicated, may hold values from -0.875 to 0.875
- ln_gain: float32 [1536], replicated, may hold values from 0.25 to 1.75
- w_expand: bfloat16 [1536, 6144], P('enc', 'mdl'), may hold values from -0.15625 to 0.15625
- w_contract: bfloat16 [1536, 6144], P('enc', 'mdl'), may hold values from -0.078125 to 0.078125
- layer_scale: float32 [1536], replicated, may hold values from 0.3 to 2
- tile_owner: int32 [256, 1], P('enc'), may hold values from 0 to 63
- tissue_index: int32 [64, 256], P('enc'), may hold values from 0 to 255, each once within a row
- slide_embed: bfloat16 [16384, 1536], P('enc'), may hold values from -6 to 6
- slide_gain: float32 [1536], replicated, may hold values from 0.25 to 1.75
- w_query: bfloat16 [1536, 768], P(None, 'mdl')
- w_key: bfloat16 [1536, 768], P(None, 'mdl')
- w_value: bfloat16 [1536, 768], P(None, 'mdl'), may hold values from -0.15625 to 0.15625
- w_out: bfloat16 [768, 1536], P('mdl'), may hold values from -0.21875 to 0.21875
- segment_level: int32 [16], P('mdl'), may hold values from 0 to 4, as said below
- dilate_rate: int32 [16], P('mdl'), may hold values from 1 to 8
- slide_length: int32 [1], replicated, may hold values from 8192 to 16384
Outputs:
- tile_embed: bfloat16 [256, 1536], P('enc')
- slide_out: bfloat16 [16384, 1536], P('enc', 'mdl')
The draws below stay inside these ranges and needn't reach their ends.
Inputs may be any that keep to these rules, and one draw needn't show every extreme that they name: `tissue_index`: each row is a permutation. `segment_level`: each level from 0 to 4 belongs to three or more heads.
All inputs are finite; a program needn't handle non-finite values.
Results may differ from the reference program's by a relative error of at most 0.013.
Values may be sent and summed in bfloat16 or wider, within the bound.
A program may use at most 64 MiB of HBM per device.

```python
import math
from functools import partial
import jax
import jax.numpy as jnp
import numpy as np
from jax import lax

D = 1536
FF = 6144
SIDE = 8
HEADS = 16
HD = 48
SLIDE_DEV = 256
ENC_TILES = 256
SEQ = 16384
N_ENC = 64


def drawn_normal(key):
    return jnp.clip(jax.random.normal(key, (D, HEADS * HD), jnp.float32), -6.0, 6.0) / math.sqrt(D)


def draw_w_query(key, part):
    own_key = jax.random.fold_in(key, 11)
    return drawn_normal(own_key).astype(jnp.bfloat16)


def draw_w_key(key, part):
    own_key = jax.random.fold_in(key, 12)
    return drawn_normal(own_key).astype(jnp.bfloat16)


def draw_segment_level(key, part):
    key = jax.random.fold_in(key, 3)
    order = jax.random.permutation(key, HEADS)
    return (order % 5).astype(jnp.int32)


def plant(entries, key, low, high):
    longest = entries.shape.index(max(entries.shape))
    spots = []
    for shift in (0, 1):
        where = [jax.random.randint(jax.random.fold_in(key, axis), (), 0, length) for axis, length in enumerate(entries.shape)]
        where[longest] = (where[longest] + shift) % entries.shape[longest]
        spots.append(tuple(where))
    return entries.at[spots[0]].set(low).at[spots[1]].set(high)


def level_of(rng, extent, pieces, least, top_value):
    def one(position, shards_of):
        draws = jax.random.uniform(jax.random.fold_in(jax.random.fold_in(rng, 6), position), (shards_of,), jnp.float32, least / len(pieces), top_value / len(pieces))
        return jnp.repeat(jnp.exp(draws), extent[position] // shards_of).reshape((-1,) + (1,) * (len(extent) - position - 1))

    loudness = one(*pieces[0])
    for cut in pieces[1:]:
        loudness = loudness * one(*cut)
    return loudness


def rank_table(count, lean):
    loads = [(1 << 20) // math.isqrt(rank ** lean) + 1 for rank in range(1, count + 1)]
    scale = 1 + sum(loads) // (1 << 30)
    return np.cumsum(np.array([max(1, weight // scale) for weight in loads]))


def skewed_ids(key, dims, number_of, lean):
    listing = rank_table(number_of, lean)
    pick = jax.random.randint(jax.random.fold_in(key, 1), dims, 0, int(listing[number_of - 1]))
    rank = jnp.searchsorted(jnp.asarray(listing, jnp.int32), pick, side="right")
    return jax.random.permutation(jax.random.fold_in(key, 2), number_of)[rank].astype(jnp.int32)


def gaussian(rng, extent, deviation, reach, cuts=(), kind=jnp.bfloat16):
    entries = deviation * jax.random.normal(rng, extent, jnp.float32)
    if cuts:
        entries = entries * level_of(rng, extent, cuts, -0.22, 0.18)
    return jnp.clip(entries, -reach, reach).astype(kind)


def setup_inputs(seed: int = 0) -> dict:
    streams_of = jax.random.split(jax.random.key(seed), 18)
    tile_feats = gaussian(streams_of[0], (ENC_TILES, SIDE, SIDE, D), 1.0, 6.0, ((0, 64),))
    dw_weight = gaussian(streams_of[1], (7, 7, D), 49 ** -0.5, 0.875)
    ln_gain = jnp.clip(1.0 + 0.15 * jax.random.normal(streams_of[2], (D,), jnp.float32), 0.25, 1.75)
    w_expand = gaussian(streams_of[3], (D, FF), D ** -0.5, 0.15625, ((0, 64), (1, 8)))
    w_contract = gaussian(streams_of[4], (D, FF), FF ** -0.5, 0.078125, ((0, 64), (1, 8)))
    layer_scale = jnp.clip(jnp.exp(jax.random.uniform(streams_of[5], (D,), jnp.float32, math.log(0.3), math.log(2.0))), 0.3, 2.0)
    tile_owner = plant(skewed_ids(streams_of[6], (ENC_TILES, 1), N_ENC, 2), jax.random.fold_in(streams_of[6], 3), 0, N_ENC - 1).astype(jnp.int32)
    tissue_index = jax.vmap(lambda own: jax.random.permutation(own, SLIDE_DEV))(jax.random.split(streams_of[7], N_ENC)).reshape((N_ENC, SLIDE_DEV)).astype(jnp.int32)
    slide_embed = gaussian(streams_of[8], (SEQ, D), 1.0, 6.0, ((0, 64),))
    slide_gain = jnp.clip(1.0 + 0.15 * jax.random.normal(streams_of[9], (D,), jnp.float32), 0.25, 1.75)
    w_query = draw_w_query(jax.random.fold_in(streams_of[17], 71), 0)
    w_key = draw_w_key(jax.random.fold_in(streams_of[17], 71), 0)
    w_value = gaussian(streams_of[12], (D, HEADS * HD), D ** -0.5, 0.15625, ((1, 8),))
    w_out = gaussian(streams_of[13], (HEADS * HD, D), (HEADS * HD) ** -0.5, 0.21875, ((0, 8),))
    segment_level = draw_segment_level(jax.random.fold_in(streams_of[17], 71), 0)
    dilate_rate = plant(jax.random.randint(streams_of[15], (HEADS,), 1, 9), jax.random.fold_in(streams_of[15], 1), 1, 8).astype(jnp.int32)
    slide_length = jax.random.randint(streams_of[16], (1,), SEQ // 2, SEQ + 1).astype(jnp.int32)
    return {"tile_feats": tile_feats, "dw_weight": dw_weight, "ln_gain": ln_gain, "w_expand": w_expand, "w_contract": w_contract, "layer_scale": layer_scale, "tile_owner": tile_owner, "tissue_index": tissue_index, "slide_embed": slide_embed, "slide_gain": slide_gain, "w_query": w_query, "w_key": w_key, "w_value": w_value, "w_out": w_out, "segment_level": segment_level, "dilate_rate": dilate_rate, "slide_length": slide_length}


def depthwise(tiles, kernel):
    side = tiles.shape[1]
    padded = jnp.pad(tiles.astype(jnp.float32), ((0, 0), (3, 3), (3, 3), (0, 0)))
    weight = kernel.astype(jnp.float32)
    total = jnp.zeros(tiles.shape, jnp.float32)
    for row in range(7):
        for col in range(7):
            total = total + padded[:, row:row + side, col:col + side, :] * weight[row, col]
    return total

def layer_norm(values, gain, epsilon):
    center = values - lax.optimization_barrier(jnp.mean(values, axis=-1, keepdims=True))
    spread = lax.optimization_barrier(jnp.mean(center * center, axis=-1, keepdims=True))
    return center * lax.rsqrt(spread + epsilon) * gain

def attend_head(q_head, k_head, v_head, rate, length, seg_size):
    scale = 1.0 / HD ** 0.5

    def one_block(block):
        first = (block * SLIDE_DEV).astype(jnp.int32)
        q_block = lax.dynamic_slice_in_dim(q_head, first, SLIDE_DEV, 0)
        begin = (first // seg_size * seg_size).astype(jnp.int32)
        k_block = lax.dynamic_slice_in_dim(k_head, begin, seg_size, 0)
        v_block = lax.dynamic_slice_in_dim(v_head, begin, seg_size, 0)
        q_index = first + jnp.arange(SLIDE_DEV, dtype=jnp.int32)
        k_index = begin + jnp.arange(seg_size, dtype=jnp.int32)
        visible = (q_index[:, None] % rate == k_index[None, :] % rate) & (k_index[None, :] < length)
        scores = jnp.dot(q_block, k_block.T, preferred_element_type=jnp.float32) * scale
        scores = jnp.where(visible, scores, -1e+30)
        top = lax.optimization_barrier(jnp.max(scores, axis=1, keepdims=True))
        weights = jnp.where(visible, jnp.exp(scores - top), 0.0)
        total = lax.optimization_barrier(jnp.sum(weights, axis=1, keepdims=True))
        summed = jnp.dot(weights.astype(jnp.bfloat16), v_block, preferred_element_type=jnp.float32)
        live = q_index[:, None] < length
        return jnp.where(live, summed / jnp.where(total > 0, total, 1.0), 0.0)
    blocks = lax.map(one_block, jnp.arange(SEQ // SLIDE_DEV, dtype=jnp.int32))
    return blocks.reshape(SEQ, HD)

def reference(tile_feats, dw_weight, ln_gain, w_expand, w_contract, layer_scale, tile_owner, tissue_index, slide_embed, slide_gain, w_query, w_key, w_value, w_out, segment_level, dilate_rate, slide_length):
    conv = depthwise(tile_feats, dw_weight)
    normed = layer_norm(conv, ln_gain, 1e-06).astype(jnp.bfloat16).reshape(-1, D)
    hidden = jax.nn.gelu(jnp.dot(normed, w_expand, preferred_element_type=jnp.float32), approximate=False).astype(jnp.bfloat16)
    mixed = lax.dot_general(hidden, w_contract, (((1,), (1,)), ((), ())), preferred_element_type=jnp.float32)
    mixed = mixed.reshape(tile_feats.shape)
    fresh = lax.optimization_barrier(jnp.mean(tile_feats.astype(jnp.float32) + layer_scale * mixed, axis=(1, 2))).astype(jnp.bfloat16)
    owner_flat = tile_owner[:, 0].astype(jnp.int32)
    slot = jnp.arange(ENC_TILES, dtype=jnp.int32)
    target = (owner_flat * SLIDE_DEV + tissue_index[owner_flat, slot]).astype(jnp.int32)
    strip = slide_embed.at[target].set(fresh)
    snorm = layer_norm(strip.astype(jnp.float32), slide_gain, 1e-05).astype(jnp.bfloat16)
    query = jnp.dot(snorm, w_query, preferred_element_type=jnp.float32).astype(jnp.bfloat16).reshape(SEQ, HEADS, HD)
    key = jnp.dot(snorm, w_key, preferred_element_type=jnp.float32).astype(jnp.bfloat16).reshape(SEQ, HEADS, HD)
    value = jnp.dot(snorm, w_value, preferred_element_type=jnp.float32).astype(jnp.bfloat16).reshape(SEQ, HEADS, HD)
    length = slide_length[0]
    branches = [partial(attend_head, seg_size=SEQ >> level_count) for level_count in range(5)]

    def one_head(head):
        return lax.switch(segment_level[head], branches, query[:, head, :], key[:, head, :], value[:, head, :], dilate_rate[head], length)
    heads_out = lax.map(one_head, jnp.arange(HEADS, dtype=jnp.int32))
    attn = jnp.transpose(heads_out, (1, 0, 2)).reshape(SEQ, HEADS * HD).astype(jnp.bfloat16)
    projected = jnp.dot(attn, w_out, preferred_element_type=jnp.float32)
    slide_out = (strip.astype(jnp.float32) + projected).astype(jnp.bfloat16)
    return (fresh, slide_out)
```

```python
import functools
import math

import jax
import jax.numpy as jnp
from jax import lax
from jax.experimental import pallas as pl
from jax.experimental.pallas import tpu as pltpu
from jax.sharding import PartitionSpec as P

MESH = pl.DeviceIdType.MESH
F32 = jnp.float32
BF16 = jnp.bfloat16
HD = 48
D = 1536
NEG = -1e30
NY, NX, NZ = 8, 4, 8


def wrap(v, n):
    return lax.rem(v + 2 * n, n)


def place():
    e = lax.axis_index("enc")
    m = lax.axis_index("mdl")
    return e, m, lax.rem(e, 2), lax.rem(e // 2, NX), e // (2 * NX)


def device(y, x, c, m):
    return (y * (2 * NX) + x * 2 + c, m)


class Gather:
    def __init__(self, wave, buf, sems, split, share):
        self.w, self.buf, self.split, self.share = wave, buf, split, share
        self.send, self.recv, self.dsend, self.drecv = sems
        self.e, self.m, self.c, self.x, self.y = place()

    def half(self, core, y, x, h):
        ref = self.at(core, y, x)
        if self.split is None:
            return ref if h == 0 else None
        rows = self.buf.shape[3]
        return ref.at[pl.ds(0, self.split)] if h == 0 else ref.at[pl.ds(self.split, rows - self.split)]

    def at(self, core, y, x):
        return self.buf.at[core if self.share else 0, y, x]

    def own(self):
        return (self.c if self.share else 0, self.y, self.x)

    def pieces(self, core, s):
        x, y, m = self.x, self.y, self.m
        out = []
        for d, sg in ((0, 1), (1, -1)):
            wx = lambda k: wrap(x - k * sg, NX)
            wy = lambda k: wrap(y - k * sg, NY)
            if core == 0:
                if s < 2:
                    to = device(y, wx(-1), 0, m)
                    if s == 0:
                        p, q = self.at(0, y, x), self.at(0, y, wx(1))
                    else:
                        p, q = self.half(0, y, wx(1), d), self.half(0, y, wx(2), d)
                else:
                    k = s - 2
                    to = device(wy(-1), x, 0, m)
                    if k < 3:
                        p, q = self.at(0, wy(k), pl.ds(0, 4)), self.at(0, wy(k + 1), pl.ds(0, 4))
                    else:
                        p, q = self.at(0, wy(k), pl.ds(2 * d, 2)), self.at(0, wy(k + 1), pl.ds(2 * d, 2))
            else:
                if s < 4:
                    to = device(wy(-1), x, 1, m)
                    if s < 3:
                        p, q = self.at(1, wy(s), x), self.at(1, wy(s + 1), x)
                    else:
                        p, q = self.half(1, wy(s), x, d), self.half(1, wy(s + 1), x, d)
                else:
                    k = s - 4
                    to = device(y, wx(-1), 1, m)
                    if k < 1:
                        p, q = self.at(1, pl.ds(0, 8), x), self.at(1, pl.ds(0, 8), wx(1))
                    else:
                        p, q = self.at(1, pl.ds(4 * d, 4), wx(1)), self.at(1, pl.ds(4 * d, 4), wx(2))
            if p is not None:
                out.append((d, p, q, to))
        return out

    def remote(self, ref, s, d, to):
        return pltpu.make_async_remote_copy(
            src_ref=ref, dst_ref=ref, send_sem=self.send.at[self.w, s, d], recv_sem=self.recv.at[self.w, s, d],
            device_id=to, device_id_type=MESH)

    def shared(self, core):
        x, y = self.x, self.y
        if core == 0:
            b = lambda k: self.at(0, wrap(y + k, NY), pl.ds(0, 4))
            return {2: [b(0)], 3: [b(-1), b(1)], 4: [b(-2), b(2)], 5: [b(-3), b(3)], 6: [b(4)]}
        b = lambda k: self.at(1, pl.ds(0, 8), wrap(x + k, NX))
        return {4: [b(0)], 5: [b(-1), b(1)], 6: [b(2)]}

    def share_copies(self, core):
        to = device(self.y, self.x, 1 - core, self.m)
        out, k = {}, 0
        for s, refs in self.shared(core).items():
            out[s] = []
            for ref in refs:
                out[s].append(pltpu.make_async_remote_copy(
                    src_ref=ref, dst_ref=ref, send_sem=self.dsend.at[self.w, k], recv_sem=self.drecv.at[self.w, k],
                    device_id=to, device_id_type=MESH))
                k += 1
        return out

    def step(self, s):
        for core in (0, 1):

            @pl.when(self.c == core)
            def _():
                if s > 0:
                    for d, _, q, to in self.pieces(core, s - 1):
                        self.remote(q, s - 1, d, to).wait_recv()
                if s < 6:
                    for d, p, _, to in self.pieces(core, s):
                        self.remote(p, s, d, to).start()
                if self.share:
                    for copy in self.share_copies(core).get(s, []):
                        copy.start()

    def drain(self):
        for core in (0, 1):

            @pl.when(self.c == core)
            def _():
                for s in range(6):
                    for d, p, _, to in self.pieces(core, s):
                        self.remote(p, s, d, to).wait_send()
                if self.share:
                    for copies in self.share_copies(core).values():
                        for copy in copies:
                            copy.wait_send()
                    for copies in self.share_copies(1 - core).values():
                        for copy in copies:
                            copy.wait_recv()


def z_copies(src, dst, send, recv, first):
    e, m, _, _, _ = place()
    out = []
    for j in range(1, NZ):
        to, back = wrap(m + j, NZ), wrap(m - j, NZ)
        mk = lambda s, d: pltpu.make_async_remote_copy(
            src_ref=s, dst_ref=d, send_sem=send.at[first + j - 1], recv_sem=recv.at[first + j - 1],
            device_id=(e, to), device_id_type=MESH)
        out.append((mk(src(to), dst.at[m]), mk(src(to), dst.at[back])))
    return out


def greet(targets):
    barrier = pltpu.get_barrier_semaphore()
    for to in targets:
        pl.semaphore_signal(barrier, inc=1, device_id=to, device_id_type=MESH)
    pl.semaphore_wait(barrier, len(targets))


def normed_rows(values, gain, epsilon):
    center = values - jnp.mean(values, axis=-1, keepdims=True)
    spread = jnp.mean(center * center, axis=-1, keepdims=True)
    return center * lax.rsqrt(spread + epsilon) * gain


def encode(feats, dw, lng, we, wc, ls, own, tissue, slide, sg, wk, wv, wo,
           emb, kvb, metab, fb, wor,
           wxs, wxr, wb, wcb, nb, conv, mf, dxs, dxr, zs, zr, exs, exr, ws,
           send, recv, dsend, drecv, msend, mrecv):
    e, m, c, x, y = place()
    other = device(y, x, 1 - c, m)
    targets = [other]
    for sg_ in (1, -1):
        targets.append(device(y, wrap(x + sg_, NX), c, m))
        targets.append(device(wrap(y + sg_, NY), x, c, m))
    for j in range(1, NZ):
        targets.append((e, wrap(m + j, NZ)))
    greet(targets)
    sems = (send, recv, dsend, drecv)

    def across(src, dst, k):
        return pltpu.make_async_remote_copy(
            src_ref=src, dst_ref=dst, send_sem=msend.at[k], recv_sem=mrecv.at[k], device_id=other, device_id_type=MESH)

    for core in (0, 1):

        @pl.when(c == core)
        def _():
            lanes = pl.ds(384 * (1 - core), 384)
            wxs[0] = we[:, lanes].astype(F32)
            wxs[1] = wc[:, lanes].astype(F32)

    cross_w = across(wxs, wxr, 0)
    cross_w.start()

    snorm = normed_rows(slide[...].astype(F32), sg[...], 1e-05).astype(BF16)
    g_kv = Gather(2, kvb, sems, 96, True)
    for i, ref in enumerate((wk, wv)):
        rows = jnp.dot(snorm, ref[...], preferred_element_type=F32)
        kvb[c, y, x, pl.ds(96 * i, 96), :] = rows.T.astype(BF16)

    g_meta = Gather(3, metab, sems, None, True)
    row = lax.broadcasted_iota(jnp.int32, (16, 128), 0)
    lane = lax.broadcasted_iota(jnp.int32, (16, 128), 1)
    info = jnp.where(row == 0, tissue[:, pl.ds(0, 128)].astype(F32), 0.0)
    info = jnp.where(row == 1, tissue[:, pl.ds(128, 128)].astype(F32), info)
    for i in range(4):
        info = jnp.where((row - 2) * 128 + lane == 4 * e + i, own[i, 0].astype(F32), info)
    metab[c, y, x] = info.astype(BF16)

    cross_w.wait()
    g_w = Gather(0, wb, sems, 16, False)
    g_wc = Gather(1, wcb, sems, 32, False)
    for core in (0, 1):

        @pl.when(c == core)
        def _():
            lanes = pl.ds(384 * core, 384)
            for k, (src, dst) in enumerate(((we, wb), (wc, wcb))):
                mine = src[:, lanes].astype(F32)
                pair = [mine, wxr[k]] if core == 0 else [wxr[k], mine]
                dst[0, y, x] = jnp.concatenate(pair, axis=0).astype(BF16)

    g_w.step(0)
    g_wc.step(0)
    g_kv.step(0)
    g_meta.step(0)

    for j in range(NZ):
        ws[j] = wo[:, 192 * j:192 * j + 192]
    wor[m] = ws[m]
    wo_copies = z_copies(lambda to: ws.at[to], wor, msend, mrecv, 16)
    for copy, _ in wo_copies:
        copy.start()

    sub = lax.broadcasted_iota(jnp.int32, (8, 8, 128), 1)

    def conv_tile(t):
        def chunk(k, carry):
            lanes = pl.ds(pl.multiple_of(k * 128, 128), 128)
            xs = feats[t, :, :, lanes].astype(F32)
            mf[pl.ds(t, 1), lanes] = jnp.sum(jnp.sum(xs, axis=0), axis=0, keepdims=True)
            weight = dw[:, :, lanes].astype(F32)
            total = [jnp.zeros((8, 128), F32)] * 8
            for col in range(7):
                off = col - 3
                if off == 0:
                    moved = xs
                else:
                    moved = pltpu.roll(xs, (-off) % 8, axis=1)
                    moved = jnp.where((sub + off >= 0) & (sub + off < 8), moved, 0.0)
                for r in range(7):
                    tap = weight[r, col:col + 1, :]
                    for h in range(8):
                        if 0 <= h + r - 3 < 8:
                            total[h] = total[h] + moved[h + r - 3] * tap
            for h in range(8):
                conv[pl.ds(8 * h, 8), lanes] = total[h]
            return carry

        lax.fori_loop(0, D // 128, chunk, 0)
        nb[c, pl.ds(64 * t, 64), :] = normed_rows(conv[...], lng[...], 1e-06).astype(BF16)

    def cross_n(t):
        ref = nb.at[c, pl.ds(64 * t, 64)]
        return across(ref, ref, 1 + t)

    for t in range(4):
        conv_tile(t)
        cross_n(t).start()
        for g in (g_w, g_wc):
            g.step(t + 1)
        if t < 2:
            g_kv.step(t + 1)
            g_meta.step(t + 1)
    for s in (5, 6):
        g_w.step(s)
        g_wc.step(s)
    for s in (3,):
        g_kv.step(s)
        g_meta.step(s)

    for t in range(4):
        cross_n(t).wait_send()
        ref = nb.at[1 - c, pl.ds(64 * t, 64)]
        across(ref, ref, 1 + t).wait_recv()

    sums = []
    wfull = wb[0].reshape(D, 384)
    for k in range(4):
        pre = jnp.dot(nb[k // 2, pl.ds(128 * (k % 2), 128), :], wfull, preferred_element_type=F32)
        act = (0.5 * pre * (1.0 + lax.erf(pre * (0.5 ** 0.5)))).astype(BF16).astype(F32)
        for i in range(2):
            sums.append(jnp.sum(act[64 * i:64 * i + 64], axis=0, keepdims=True))
    hsum = jnp.concatenate(sums, axis=0)
    high = hsum.astype(BF16)
    low = (hsum - high.astype(F32)).astype(BF16)
    part = lax.dot_general(high, wcb[0].reshape(D, 384), (((1,), (1,)), ((), ())), preferred_element_type=F32)
    part += lax.dot_general(low, wcb[0].reshape(D, 384), (((1,), (1,)), ((), ())), preferred_element_type=F32)
    part = part * (ls[...] * (1.0 / 64.0))
    mine = mf[...] * (1.0 / 512.0)
    for core in (0, 1):

        @pl.when(c == core)
        def _():
            blank = jnp.zeros((4, D), F32)
            both = part + jnp.concatenate([mine, blank] if core == 0 else [blank, mine], axis=0)
            zs[...] = both[:, 768 * core:768 * core + 768]
            dxs[...] = both[:, 768 * (1 - core):768 * (1 - core) + 768]

    cross_p = across(dxs, dxr, 5)
    cross_p.start()
    g_kv.step(4)
    g_meta.step(4)
    cross_p.wait()
    zs[...] = zs[...] + dxr[...]
    zr[m] = zs[...]
    zc = z_copies(lambda to: zs, zr, msend, mrecv, 8)
    for copy, _ in zc:
        copy.start()
    g_kv.step(5)
    g_meta.step(5)
    for copy, back in zc:
        copy.wait_send()
        back.wait_recv()
    fresh = jnp.sum(zr[...], axis=0)
    exs[...] = fresh
    cross_e = across(exs, exr, 6)
    cross_e.start()
    fb[c, y, x] = jnp.concatenate([fresh[:, :384], fresh[:, 384:]], axis=0).astype(BF16)
    g_f = Gather(4, fb, sems, None, True)
    g_f.step(0)
    g_kv.step(6)
    g_meta.step(6)
    for s in range(1, 7):
        g_f.step(s)
    cross_e.wait()
    for core in (0, 1):

        @pl.when(c == core)
        def _():
            rows = pl.ds(4 * core, 4)
            emb[:, pl.ds(768 * core, 768)] = exs[rows, :].astype(BF16)
            emb[:, pl.ds(768 * (1 - core), 768)] = exr[rows, :].astype(BF16)

    for copy, back in wo_copies:
        copy.wait_send()
        back.wait_recv()
    for g in (g_w, g_wc, g_kv, g_meta, g_f):
        g.drain()


def attend(level, rate, length, place_ref, kvb, metab, fb, tissue, slide, sg, wq, wk, wv, attn, own_cols, fresh_ref, code_ref):
    e, m = place_ref[0], place_ref[1]
    seq = 16384
    n = length[0]
    for c in range(2):
        for h in range(2):
            lanes = pl.ds(768 * c + 384 * h, 384)
            block = fb[c].reshape(32, 16, 384).astype(F32)[:, 8 * h:8 * h + 8, :]
            fresh_ref[:, lanes] = block.reshape(256, 384).astype(BF16)
    fresh = fresh_ref[...]

    info = [metab[c].reshape(32, 16, 128).astype(F32) for c in range(2)]
    owner = jnp.concatenate([sum(jnp.sum(i[:, 2 + k, :], axis=0, keepdims=True) for i in info) for k in range(2)], axis=1)
    strip_of = 2 * lax.broadcasted_iota(jnp.int32, (32, 256), 0)
    picks, spots = [], 0.0
    for c in range(2):
        rows = jnp.concatenate([info[c][:, 0, :], info[c][:, 1, :]], axis=1)
        pick = ((strip_of + c).astype(F32) == owner).astype(F32)
        picks.append(pick.astype(BF16))
        spots = spots + jnp.sum(pick * rows, axis=0, keepdims=True)
    row_id = lax.broadcasted_iota(jnp.int32, (256, 256), 0).astype(F32)
    at_row = row_id == spots
    at_row_bf = at_row.astype(F32).astype(BF16)
    gone = [lax.dot_general(p, at_row_bf, (((1,), (1,)), ((), ())), preferred_element_type=F32) for p in picks]
    code_ref[0] = gone[0]
    code_ref[1] = gone[1]

    hits = (at_row & (owner == e.astype(F32))).astype(F32)
    covered = jnp.sum(hits, axis=1, keepdims=True) > 0.5
    placed = jnp.dot(hits.astype(BF16), fresh, preferred_element_type=F32)
    strip = jnp.where(covered, placed, slide[...].astype(F32))
    for j in range(NZ):

        @pl.when(m == j)
        def _():
            own_cols[...] = strip[:, 192 * j:192 * j + 192].astype(BF16)

    snorm = normed_rows(strip, sg[...], 1e-05).astype(BF16)
    query = jnp.dot(snorm, wq[...], preferred_element_type=F32).astype(BF16)
    fnorm = normed_rows(fresh.astype(F32), sg[...], 1e-05).astype(BF16)
    fkey = jnp.dot(fnorm, wk[...], preferred_element_type=F32).T.astype(BF16)
    fval = jnp.dot(fnorm, wv[...], preferred_element_type=F32).T.astype(BF16)

    feat = lax.broadcasted_iota(jnp.int32, (32, 256), 0)
    qfeat = lax.broadcasted_iota(jnp.int32, (256, 32), 1)
    lane = lax.broadcasted_iota(jnp.int32, (1, 256), 1).astype(F32)
    qrow = lax.broadcasted_iota(jnp.int32, (256, 1), 0) + e * 256
    c2 = HD ** -0.5 * math.log2(math.e)
    for h in range(2):
        r = rate[h].astype(F32)
        shift = 14 - level[h]
        width = jnp.left_shift(jnp.int32(1), shift).astype(F32)

        def classes(pos):
            seg = jnp.floor((pos + 0.5) / width)
            res = pos - r * jnp.floor((pos + 0.5) / r)
            return res, seg

        qres, qseg = classes(qrow.astype(F32))
        qhot = ((qfeat < 8) & (qfeat.astype(F32) == qres)) | ((qfeat >= 8) & (qfeat < 24) & ((qfeat - 8).astype(F32) == qseg)) | (qfeat == 24)
        qaug = jnp.concatenate([query[:, HD * h:HD * h + HD].astype(F32), jnp.where(qhot, NEG, 0.0)], axis=1).astype(BF16)

        def features(pos, dead):
            res, seg = classes(pos)
            miss = jnp.where(feat < 8, (feat.astype(F32) != res).astype(F32), ((feat - 8).astype(F32) != seg).astype(F32))
            gone = jnp.where((pos >= n.astype(F32)) | (dead > 0.5), 1.0, 0.0)
            miss = jnp.where(feat == 24, gone, miss)
            return jnp.where(feat > 24, 0.0, miss).astype(BF16)

        def update(state, keys, vals):
            top, acc = state
            s = jnp.dot(qaug, keys, preferred_element_type=F32)
            new = jnp.maximum(top, jnp.max(s, axis=1, keepdims=True))
            p = jnp.exp2(s * c2 - new * c2).astype(BF16)
            acc = acc * jnp.exp2((top - new) * c2) + lax.dot_general(p, vals, (((1,), (1,)), ((), ())), preferred_element_type=F32)
            return new, acc

        def augmented(k, f):
            return jnp.concatenate([k, f], axis=0)

        def with_ones(v):
            return jnp.concatenate([v, jnp.ones((16, v.shape[1]), BF16)], axis=0)

        fpos = owner * 256.0 + spots
        state = (jnp.full((256, 1), NEG, F32), jnp.zeros((256, 64), F32))
        state = update(state, augmented(fkey[HD * h:HD * h + HD], features(fpos, jnp.zeros((1, 256), F32))),
                       with_ones(fval[HD * h:HD * h + HD]))

        def group(g, state):
            keys, vals = [], []
            for i in range(4):
                s = 4 * g + i
                chip = 2 * g + i // 2
                ref = kvb.at[i % 2, chip // NX, lax.rem(chip, NX)]
                dead = code_ref[i % 2, pl.ds(chip, 1), :]
                pos = lane + (s * 256).astype(F32)
                keys.append(augmented(ref[pl.ds(HD * h, HD), :], features(pos, dead)))
                vals.append(with_ones(ref[pl.ds(96 + HD * h, HD), :]))
            return update(state, jnp.concatenate(keys, axis=1), jnp.concatenate(vals, axis=1))

        groups = jnp.right_shift(jnp.int32(16), level[h])
        first = e // 4 // groups * groups
        last = jnp.minimum(first + groups, (n + 1023) // 1024)
        top, acc = lax.fori_loop(first, last, group, state)
        total = acc[:, HD:HD + 1]
        out = acc[:, :HD] / jnp.where(total > 0, total, 1.0)
        out = jnp.where(qrow < n, out, 0.0)
        attn[pl.ds(HD * h, HD), :] = out.T.astype(BF16)


def project(attn, wor, own_cols, out, ab, msend, mrecv):
    e, m, c, x, y = place()
    greet([(e, wrap(m + j, NZ)) for j in range(1, NZ)])
    ab[m] = attn[...]
    copies = z_copies(lambda to: attn, ab, msend, mrecv, 0)
    for copy, _ in copies:
        copy.start()
    for copy, back in copies:
        copy.wait_send()
        back.wait_recv()
    total = lax.dot_general(ab[...].reshape(768, 256), wor[...].reshape(768, 192), (((0,), (0,)), ((), ())), preferred_element_type=F32)
    out[...] = (own_cols[...].astype(F32) + total).astype(BF16)


VM = pl.BlockSpec(memory_space=pltpu.VMEM)
SM = pl.BlockSpec(memory_space=pltpu.SMEM)


def shape(dims, dtype=BF16):
    return jax.ShapeDtypeStruct(dims, dtype)


def body(tile_feats, dw_weight, ln_gain, w_expand, w_contract, layer_scale, tile_owner, tissue_index, slide_embed,
         slide_gain, w_query, w_key, w_value, w_out, segment_level, dilate_rate, slide_length):
    dma = pltpu.SemaphoreType.DMA
    lng, ls, sg = ln_gain.reshape(1, D), layer_scale.reshape(1, D), slide_gain.reshape(1, D)
    emb, kvb, metab, fb, wor = pl.pallas_call(
        encode,
        out_shape=[shape((4, D)), shape((2, 8, 4, 192, 256)), shape((2, 8, 4, 16, 128)), shape((2, 8, 4, 16, 384)), shape((8, 96, 192))],
        in_specs=[VM] * 6 + [SM] + [VM] * 6,
        out_specs=[VM] * 5,
        scratch_shapes=[
            pltpu.VMEM((2, 24, 384), F32), pltpu.VMEM((2, 24, 384), F32),
            pltpu.VMEM((1, 8, 4, 48, 384), BF16), pltpu.VMEM((1, 8, 4, 48, 384), BF16),
            pltpu.VMEM((2, 256, D), BF16), pltpu.VMEM((64, D), F32), pltpu.VMEM((4, D), F32),
            pltpu.VMEM((8, 768), F32), pltpu.VMEM((8, 768), F32), pltpu.VMEM((8, 768), F32), pltpu.VMEM((8, 8, 768), F32),
            pltpu.VMEM((8, 768), F32), pltpu.VMEM((8, 768), F32), pltpu.VMEM((8, 96, 192), BF16),
            dma((5, 6, 2)), dma((5, 6, 2)), dma((5, 8)), dma((5, 8)), dma((24,)), dma((24,)),
        ],
        name="encode",
        compiler_params=pltpu.CompilerParams(collective_id=0, has_side_effects=True, vmem_limit_bytes=48 * 2**20),
    )(tile_feats, dw_weight, lng, w_expand, w_contract, ls, tile_owner, tissue_index, slide_embed, sg, w_key, w_value, w_out)
    here = jnp.stack([lax.axis_index("enc"), lax.axis_index("mdl")]).astype(jnp.int32)
    attn, own_cols = pl.pallas_call(
        attend,
        out_shape=[shape((96, 256)), shape((256, 192))],
        in_specs=[SM] * 4 + [VM] * 9,
        out_specs=[VM] * 2,
        scratch_shapes=[pltpu.VMEM((256, D), BF16), pltpu.VMEM((2, 32, 256), F32)],
        name="attend",
        compiler_params=pltpu.CompilerParams(vmem_limit_bytes=48 * 2**20),
    )(segment_level, dilate_rate, slide_length, here, kvb, metab, fb, tissue_index, slide_embed, sg, w_query, w_key, w_value)
    slide_out = pl.pallas_call(
        project,
        out_shape=shape((256, 192)),
        in_specs=[VM] * 3,
        out_specs=VM,
        scratch_shapes=[pltpu.VMEM((8, 96, 256), BF16), dma((7,)), dma((7,))],
        name="project",
        compiler_params=pltpu.CompilerParams(collective_id=1, has_side_effects=True, vmem_limit_bytes=32 * 2**20),
    )(attn, wor, own_cols)
    return emb, slide_out


def solution(mesh):
    placed = (
        P("enc", None, None, None),
        P(),
        P(),
        P("enc", "mdl"),
        P("enc", "mdl"),
        P(),
        P("enc", None),
        P("enc", None),
        P("enc", None),
        P(),
        P(None, "mdl"),
        P(None, "mdl"),
        P(None, "mdl"),
        P("mdl", None),
        P("mdl"),
        P("mdl"),
        P(),
    )
    return jax.shard_map(
        body,
        mesh=mesh,
        in_specs=placed,
        out_specs=(P("enc", None), P("enc", "mdl")),
        check_vma=False,
    )
```

```python
import functools
import math

import jax
import jax.numpy as jnp
from jax import lax
from jax.experimental import pallas as pl
from jax.experimental.pallas import tpu as pltpu
from jax.sharding import PartitionSpec as P

MESH = pl.DeviceIdType.MESH
F32 = jnp.float32
BF16 = jnp.bfloat16
HD = 48
D = 1536
NEG = -1e30
NY, NX, NZ = 8, 4, 8


def wrap(v, n):
    return lax.rem(v + 2 * n, n)


def place():
    e = lax.axis_index("enc")
    m = lax.axis_index("mdl")
    return e, m, lax.rem(e, 2), lax.rem(e // 2, NX), e // (2 * NX)


def device(y, x, c, m):
    return (y * (2 * NX) + x * 2 + c, m)


class Gather:
    def __init__(self, wave, buf, sems, orders, direct, split=None, share=""):
        self.w, self.buf, self.orders, self.direct, self.split, self.share = wave, buf, orders, direct, split, share
        self.send, self.recv, self.dsend, self.drecv = sems
        self.e, self.m, self.c, self.x, self.y = place()

    def at(self, core, y, x):
        return self.buf.at[core if self.share else 0, y, x]

    def own(self):
        return (self.c if self.share else 0, self.y, self.x)

    def plan(self, core):
        first, second = self.orders[core]
        size = {"x": NX, "y": NY}
        n1, n2 = size[first], size[second]

        def go(axis, k):
            if axis == "x":
                return device(self.y, wrap(self.x + k, NX), core, self.m)
            return device(wrap(self.y + k, NY), self.x, core, self.m)

        p1, p2 = (self.x, self.y) if first == "x" else (self.y, self.x)

        def ref(i1, i2):
            return self.at(core, i2, i1) if first == "x" else self.at(core, i1, i2)

        steps = []
        if self.direct[core][0]:
            steps.append([(k - 1, ref(p1, p2), ref(wrap(p1 - k, n1), p2), go(first, k)) for k in range(1, n1)])
        else:
            for s in range(n1 // 2):
                step = []
                for d, sg in ((0, 1), (1, -1)):
                    p, q = ref(wrap(p1 - s * sg, n1), p2), ref(wrap(p1 - (s + 1) * sg, n1), p2)
                    if s == n1 // 2 - 1:
                        rows = self.buf.shape[3]
                        cut = pl.ds(0, self.split) if d == 0 else pl.ds(self.split, rows - self.split)
                        p, q = p.at[cut], q.at[cut]
                    step.append((d, p, q, go(first, sg)))
                steps.append(step)
        whole = pl.ds(0, n1)
        shared = {len(steps): [ref(whole, p2)]}
        if self.direct[core][1]:
            steps.append([(k - 1, ref(whole, p2), ref(whole, wrap(p2 - k, n2)), go(second, k)) for k in range(1, n2)])
        else:
            for s in range(n2 // 2):
                step = []
                last = s == n2 // 2 - 1
                for d, sg in ((0, 1), (1, -1)):
                    part = pl.ds(d * (n1 // 2), n1 // 2) if last else whole
                    step.append((d, ref(part, wrap(p2 - s * sg, n2)), ref(part, wrap(p2 - (s + 1) * sg, n2)), go(second, sg)))
                steps.append(step)
                far = [wrap(p2 + s + 1, n2)] if last else [wrap(p2 - s - 1, n2), wrap(p2 + s + 1, n2)]
                shared[len(steps)] = [ref(whole, k) for k in far]
        if self.share == "end":
            shared = {len(steps): [self.buf.at[core]]}
        return steps, (shared if self.share else {})

    def remote(self, ref, s, k, to):
        return pltpu.make_async_remote_copy(
            src_ref=ref, dst_ref=ref, send_sem=self.send.at[self.w, s, k], recv_sem=self.recv.at[self.w, s, k],
            device_id=to, device_id_type=MESH)

    def across(self, ref, k, core):
        return pltpu.make_async_remote_copy(
            src_ref=ref, dst_ref=ref, send_sem=self.dsend.at[self.w, k], recv_sem=self.drecv.at[self.w, k],
            device_id=device(self.y, self.x, 1 - core, self.m), device_id_type=MESH)

    def step(self, s):
        for core in (0, 1):
            steps, shared = self.plan(core)
            if s > len(steps):
                continue

            @pl.when(self.c == core)
            def _():
                if s > 0:
                    for k, _, q, to in steps[s - 1]:
                        self.remote(q, s - 1, k, to).wait_recv()
                if s < len(steps):
                    for k, p, _, to in steps[s]:
                        self.remote(p, s, k, to).start()
                k = 0
                for t, refs in shared.items():
                    for ref in refs:
                        if t == s:
                            self.across(ref, k, core).start()
                        k += 1

    def finish(self):
        for core in (0, 1):
            _, shared = self.plan(1 - core)

            @pl.when(self.c == core)
            def _():
                for k, ref in enumerate([r for refs in shared.values() for r in refs]):
                    self.across(ref, k, core).wait_recv()

    def drain(self):
        for core in (0, 1):
            steps, shared = self.plan(core)

            @pl.when(self.c == core)
            def _():
                for s, step in enumerate(steps):
                    for k, p, _, to in step:
                        self.remote(p, s, k, to).wait_send()
                for k, ref in enumerate([r for refs in shared.values() for r in refs]):
                    self.across(ref, k, core).wait_send()


def z_copies(src, dst, send, recv, first):
    e, m, _, _, _ = place()
    out = []
    for j in range(1, NZ):
        to, back = wrap(m + j, NZ), wrap(m - j, NZ)
        mk = lambda s, d: pltpu.make_async_remote_copy(
            src_ref=s, dst_ref=d, send_sem=send.at[first + j - 1], recv_sem=recv.at[first + j - 1],
            device_id=(e, to), device_id_type=MESH)
        out.append((mk(src(to), dst.at[m]), mk(src(to), dst.at[back])))
    return out


def normed_rows(values, gain, epsilon):
    center = values - jnp.mean(values, axis=-1, keepdims=True)
    spread = jnp.mean(center * center, axis=-1, keepdims=True)
    return center * lax.rsqrt(spread + epsilon) * gain


def whole(feats_h, dw_h, lng, we_h, wc_h, ls, owner_row, tissue, slide_h, sg, wq_h, wk_h, wv_h, wo_h, level, rate, length,
          emb, out,
          feats, dw, we, wc, slide, wq, wk, wv, wo,
          wxs, wxr, wb, wcb, nb, conv, mf, dxs, dxr, zs, zr, exs, exr, ws, wor,
          kvb, metab, fb, keyf, s0, s1, fresh_ref, ab, attn,
          lsem, send, recv, dsend, drecv, msend, mrecv):
    e, m, c, x, y = place()
    other = device(y, x, 1 - c, m)
    targets = [other]
    for sg_ in range(1, NX):
        targets.append(device(y, wrap(x + sg_, NX), c, m))
    for sg_ in range(1, NY):
        targets.append(device(wrap(y + sg_, NY), x, c, m))
    for j in range(1, NZ):
        targets.append((e, wrap(m + j, NZ)))
    barrier = pltpu.get_barrier_semaphore()
    for to in targets:
        pl.semaphore_signal(barrier, inc=1, device_id=to, device_id_type=MESH)

    loads = {}
    for i, (name, src, dst) in enumerate((("we", we_h, we), ("wc", wc_h, wc), ("slide", slide_h, slide), ("wk", wk_h, wk), ("wv", wv_h, wv),
                                          ("feats", feats_h, feats), ("dw", dw_h, dw), ("wo", wo_h, wo), ("wq", wq_h, wq))):
        loads[name] = pltpu.make_async_copy(src, dst, lsem.at[i])
        loads[name].start()
    sems = (send, recv, dsend, drecv)

    def across(src, dst, k):
        return pltpu.make_async_remote_copy(
            src_ref=src, dst_ref=dst, send_sem=msend.at[k], recv_sem=mrecv.at[k], device_id=other, device_id_type=MESH)

    nt = lambda a, b: lax.dot_general(a, b, (((1,), (1,)), ((), ())), preferred_element_type=F32)

    loads["we"].wait()
    loads["wc"].wait()
    for core in (0, 1):

        @pl.when(c == core)
        def _():
            lanes = pl.ds(384 * (1 - core), 384)
            wxs[0] = we[:, lanes].astype(F32)
            wxs[1] = wc[:, lanes].astype(F32)

    loads["slide"].wait()
    loads["wk"].wait()
    loads["wv"].wait()
    gain = sg[...].reshape(1, D)
    snorm = normed_rows(slide[...].astype(F32), gain, 1e-05).astype(BF16)
    for i, ref in enumerate((wk, wv)):
        kvb[c, y, x, pl.ds(96 * i, 96), :] = nt(ref[...], snorm).astype(BF16)

    row = lax.broadcasted_iota(jnp.int32, (16, 128), 0)
    lane = lax.broadcasted_iota(jnp.int32, (16, 128), 1)
    info = jnp.where(row == 0, tissue[:, pl.ds(0, 128)].astype(F32), 0.0)
    info = jnp.where(row == 1, tissue[:, pl.ds(128, 128)].astype(F32), info)
    own = owner_row[...].astype(F32)
    for i in range(4):
        info = jnp.where((row - 2) * 128 + lane == 4 * e + i, own[:, i:i + 1], info)
    metab[c, y, x] = info.astype(BF16)

    pl.semaphore_wait(barrier, len(targets))
    cross_w = across(wxs, wxr, 0)
    cross_w.start()
    mixed = ("xy", "yx")
    g_w = Gather(0, wb, sems, mixed, ((True, False), (True, False)))
    g_wc = Gather(1, wcb, sems, mixed, ((True, False), (True, False)))
    g_kv = Gather(2, kvb, sems, mixed, ((True, False), (False, False)), 96, "step")
    g_meta = Gather(3, metab, sems, mixed, ((True, True), (True, True)), share="end")
    g_f = Gather(4, fb, sems, mixed, ((True, True), (True, True)), share="end")
    g_meta.step(0)
    cross_w.wait()
    for core in (0, 1):

        @pl.when(c == core)
        def _():
            lanes = pl.ds(384 * core, 384)
            for k, (src, dst) in enumerate(((we, wb), (wc, wcb))):
                mine = src[:, lanes].astype(F32)
                pair = [mine, wxr[k]] if core == 0 else [wxr[k], mine]
                dst[0, y, x] = jnp.concatenate(pair, axis=0).astype(BF16)

    g_w.step(0)
    g_wc.step(0)
    g_kv.step(0)

    loads["wo"].wait()
    for j in range(NZ):
        ws[j] = wo[:, 192 * j:192 * j + 192]
    wor[m] = ws[m]
    wo_copies = z_copies(lambda to: ws.at[to], wor, msend, mrecv, 16)
    for copy, _ in wo_copies:
        copy.start()

    loads["feats"].wait()
    loads["dw"].wait()
    sub = lax.broadcasted_iota(jnp.int32, (8, 8, 128), 1)

    def conv_tile(t):
        def chunk(k, carry):
            lanes = pl.ds(pl.multiple_of(k * 128, 128), 128)
            xs = feats[t, :, :, lanes].astype(F32)
            mf[pl.ds(t, 1), lanes] = jnp.sum(jnp.sum(xs, axis=0), axis=0, keepdims=True)
            weight = dw[:, :, lanes].astype(F32)
            total = [jnp.zeros((8, 128), F32)] * 8
            for col in range(7):
                off = col - 3
                if off == 0:
                    moved = xs
                else:
                    moved = pltpu.roll(xs, (-off) % 8, axis=1)
                    moved = jnp.where((sub + off >= 0) & (sub + off < 8), moved, 0.0)
                for r in range(7):
                    tap = weight[r, col:col + 1, :]
                    for h in range(8):
                        if 0 <= h + r - 3 < 8:
                            total[h] = total[h] + moved[h + r - 3] * tap
            for h in range(8):
                conv[pl.ds(8 * h, 8), lanes] = total[h]
            return carry

        lax.fori_loop(0, D // 128, chunk, 0)
        nb[c, pl.ds(64 * t, 64), :] = normed_rows(conv[...], lng[...].reshape(1, D), 1e-06).astype(BF16)

    def cross_n(t):
        ref = nb.at[c, pl.ds(64 * t, 64)]
        return across(ref, ref, 1 + t)

    after = {0: ((g_w, 1), (g_wc, 1), (g_meta, 1)), 1: ((g_w, 2), (g_wc, 2), (g_kv, 1)), 2: ((g_w, 3), (g_wc, 3), (g_meta, 2)),
             3: ((g_w, 4), (g_wc, 4), (g_kv, 2), (g_w, 5), (g_wc, 5))}
    for t in range(4):
        conv_tile(t)
        cross_n(t).start()
        for g, s in after[t]:
            g.step(s)
    g_kv.step(3)
    for t in range(4):
        cross_n(t).wait_send()
        ref = nb.at[1 - c, pl.ds(64 * t, 64)]
        across(ref, ref, 1 + t).wait_recv()

    sums = []
    wfull = wb[0].reshape(D, 384)
    for k in range(4):
        pre = jnp.dot(nb[k // 2, pl.ds(128 * (k % 2), 128), :], wfull, preferred_element_type=F32)
        act = (0.5 * pre * (1.0 + lax.erf(pre * (0.5 ** 0.5)))).astype(BF16).astype(F32)
        for i in range(2):
            sums.append(jnp.sum(act[64 * i:64 * i + 64], axis=0, keepdims=True))
    hsum = jnp.concatenate(sums, axis=0)
    high = hsum.astype(BF16)
    low = (hsum - high.astype(F32)).astype(BF16)
    part = nt(high, wcb[0].reshape(D, 384)) + nt(low, wcb[0].reshape(D, 384))
    part = part * (ls[...].reshape(1, D) * (1.0 / 64.0))
    mine = mf[...] * (1.0 / 512.0)
    for core in (0, 1):

        @pl.when(c == core)
        def _():
            blank = jnp.zeros((4, D), F32)
            both = part + jnp.concatenate([mine, blank] if core == 0 else [blank, mine], axis=0)
            zs[...] = both[:, 768 * core:768 * core + 768]
            dxs[...] = both[:, 768 * (1 - core):768 * (1 - core) + 768]

    cross_p = across(dxs, dxr, 5)
    cross_p.start()
    g_kv.step(4)
    cross_p.wait()
    zs[...] = zs[...] + dxr[...]
    zr[m] = zs[...]
    zc = z_copies(lambda to: zs, zr, msend, mrecv, 8)
    for copy, _ in zc:
        copy.start()

    g_meta.finish()
    info = [metab[k].reshape(32, 16, 128).astype(F32) for k in range(2)]
    owner = jnp.concatenate([sum(jnp.sum(i[:, 2 + k, :], axis=0, keepdims=True) for i in info) for k in range(2)], axis=1)
    strip_of = 2 * lax.broadcasted_iota(jnp.int32, (32, 256), 0)
    picks, spots = [], 0.0
    for k in range(2):
        rows = jnp.concatenate([info[k][:, 0, :], info[k][:, 1, :]], axis=1)
        pick = ((strip_of + k).astype(F32) == owner).astype(F32)
        picks.append(pick.astype(BF16))
        spots = spots + jnp.sum(pick * rows, axis=0, keepdims=True)
    row_id = lax.broadcasted_iota(jnp.int32, (256, 256), 0).astype(F32)
    at_row = row_id == spots
    at_row_bf = at_row.astype(F32).astype(BF16)
    gone = [nt(p, at_row_bf) for p in picks]

    f = lax.broadcasted_iota(jnp.int32, (32, 256), 0)
    amount = jnp.where(f < 8, 10 + f % 4, jnp.where(f < 14, (f - 8) % 3, (f - 14) % 3))
    flipped = ((f >= 4) & (f < 8)) | ((f >= 11) & (f < 14)) | ((f >= 17) & (f < 20))
    rates = [rate[h].astype(F32) for h in range(2)]
    limit = length[0].astype(F32)

    def bits(pos):
        pos_f = pos.astype(F32)
        res = [(pos_f - r * jnp.floor((pos_f + 0.5) / r)).astype(jnp.int32) for r in rates]
        src = jnp.where(f < 8, pos, jnp.where(f < 14, res[0], res[1]))
        bit = (jnp.right_shift(src, amount) & 1).astype(F32)
        return jnp.where(f < 20, jnp.where(flipped, 1.0 - bit, bit), 0.0)

    def features(pos, dead):
        dead = jnp.where(pos.astype(F32) >= limit, 1.0, dead)
        return jnp.where(f == 20, dead, bits(pos)).astype(BF16)

    line = lax.broadcasted_iota(jnp.int32, (1, 256), 1)
    for k in range(64):
        core, chip = k // 32, k % 32
        keyf[core, chip // NX, chip % NX] = features(line + (2 * chip + core) * 256, gone[core][chip:chip + 1, :])

    qpos = line + e * 256
    qbits = 1.0 - bits(qpos)
    bias = []
    for h in range(2):
        live = (f < 8) & (f % 4 >= 4 - level[h])
        live = live | ((f >= 8 + 6 * h) & (f < 14 + 6 * h)) | (f == 20)
        bias.append(jnp.where(live, qbits * NEG, 0.0).astype(BF16))

    g_kv.step(5)
    for copy, back in zc:
        copy.wait_send()
        back.wait_recv()
    fresh = jnp.sum(zr[...], axis=0)
    exs[...] = fresh
    cross_e = across(exs, exr, 6)
    cross_e.start()
    fb[c, y, x] = jnp.concatenate([fresh[:, :384], fresh[:, 384:]], axis=0).astype(BF16)
    g_f.step(0)
    cross_e.wait()
    for core in (0, 1):

        @pl.when(c == core)
        def _():
            rows = pl.ds(4 * core, 4)
            emb[:, pl.ds(768 * core, 768)] = exs[rows, :].astype(BF16)
            emb[:, pl.ds(768 * (1 - core), 768)] = exr[rows, :].astype(BF16)

    loads["wq"].wait()
    g_f.step(1)
    g_kv.step(6)
    g_f.step(2)
    g_f.finish()

    for k in range(2):
        for h in range(2):
            block = fb[k].reshape(32, 16, 384).astype(F32)[:, 8 * h:8 * h + 8, :]
            fresh_ref[:, pl.ds(768 * k + 384 * h, 384)] = block.reshape(256, 384).astype(BF16)
    rows = fresh_ref[...]
    hits = (at_row & (owner == e.astype(F32))).astype(F32)
    covered = jnp.sum(hits, axis=1, keepdims=True) > 0.5
    placed = jnp.dot(hits.astype(BF16), rows, preferred_element_type=F32)
    strip = jnp.where(covered, placed, slide[...].astype(F32))
    for j in range(NZ):

        @pl.when(m == j)
        def _():
            out[...] = strip[:, 192 * j:192 * j + 192].astype(BF16)

    c2 = HD ** -0.5 * math.log2(math.e)
    query = (nt(wq[...], normed_rows(strip, gain, 1e-05).astype(BF16)) * c2).astype(BF16)
    fnorm = normed_rows(rows.astype(F32), gain, 1e-05).astype(BF16)
    fkey = nt(wk[...], fnorm).astype(BF16)
    fval = nt(wv[...], fnorm).astype(BF16)
    ffeat = features((owner * 256.0 + spots).astype(jnp.int32), jnp.zeros((1, 256), F32))
    blank = jnp.zeros((HD, 256), BF16)
    qaug = jnp.concatenate([jnp.concatenate([query[:HD], blank, bias[0]], axis=0),
                            jnp.concatenate([blank, query[HD:], bias[1]], axis=0)], axis=1)
    g_kv.finish()

    tn = lambda a, b: lax.dot_general(a, b, (((0,), (0,)), ((), ())), preferred_element_type=F32)

    def softened(s, state, values):
        top = state[0]
        new = jnp.maximum(top, jnp.max(s, axis=0, keepdims=True))
        p = jnp.exp2(s - new).astype(BF16)
        shrink = jnp.exp2(top - new)
        acc = [state[1 + h] * shrink[:, 256 * h:256 * h + 256]
               + jnp.dot(values[h], p[:, 256 * h:256 * h + 256], preferred_element_type=F32) for h in range(2)]
        return (new, *acc)

    def score(g, ref):
        k, r = g // NY, lax.rem(g, NY)
        keys = jnp.concatenate(
            [jnp.concatenate([kvb[k, r, i, pl.ds(0, 96), :] for i in range(NX)], axis=1),
             jnp.concatenate([keyf[k, r, i] for i in range(NX)], axis=1)], axis=0)
        ref[...] = tn(keys, qaug)

    def soft(g, ref, state):
        k, r = g // NY, lax.rem(g, NY)
        values = []
        for h in range(2):
            v = jnp.concatenate([kvb[k, r, i, pl.ds(96 + HD * h, HD), :] for i in range(NX)], axis=1)
            values.append(jnp.concatenate([v, jnp.ones((16, 1024), BF16)], axis=0))
        return softened(ref[...], state, values)

    state = (jnp.full((1, 512), NEG, F32), jnp.zeros((64, 256), F32), jnp.zeros((64, 256), F32))
    state = softened(tn(jnp.concatenate([fkey, ffeat], axis=0), qaug), state,
                     [jnp.concatenate([fval[HD * h:HD * h + HD], jnp.ones((16, 256), BF16)], axis=0) for h in range(2)])
    score(0, s0)

    def two(i, state):
        score(2 * i + 1, s1)
        state = soft(2 * i, s0, state)
        score(jnp.minimum(2 * i + 2, 15), s0)
        return soft(2 * i + 1, s1, state)

    _, *acc = lax.fori_loop(0, 8, two, state)
    for h in range(2):
        total = acc[h][HD:HD + 1]
        head = acc[h][:HD] / jnp.where(total > 0, total, 1.0)
        attn[pl.ds(HD * h, HD), :] = jnp.where(qpos.astype(F32) < limit, head, 0.0).astype(BF16)

    ab[m] = attn[...]
    copies = z_copies(lambda to: attn, ab, msend, mrecv, 24)
    for copy, _ in copies:
        copy.start()
    for copy, back in wo_copies:
        copy.wait_send()
        back.wait_recv()
    for g in (g_w, g_wc, g_kv, g_meta, g_f):
        g.drain()
    for copy, back in copies:
        copy.wait_send()
        back.wait_recv()
    total = tn(ab[...].reshape(768, 256), wor[...].reshape(768, 192))
    out[...] = (out[...].astype(F32) + total).astype(BF16)


VM = pl.BlockSpec(memory_space=pltpu.VMEM)
SM = pl.BlockSpec(memory_space=pltpu.SMEM)
ANY = pl.BlockSpec(memory_space=pl.ANY)


def shape(dims, dtype=BF16):
    return jax.ShapeDtypeStruct(dims, dtype)


def body(tile_feats, dw_weight, ln_gain, w_expand, w_contract, layer_scale, tile_owner, tissue_index, slide_embed,
         slide_gain, w_query, w_key, w_value, w_out, segment_level, dilate_rate, slide_length):
    dma = pltpu.SemaphoreType.DMA
    vm = lambda dims, dtype=BF16: pltpu.VMEM(dims, dtype)
    return pl.pallas_call(
        whole,
        out_shape=[shape((4, D)), shape((256, 192))],
        in_specs=[ANY, ANY, VM, ANY, ANY, VM, VM, VM, ANY, VM, ANY, ANY, ANY, ANY, SM, SM, SM],
        out_specs=[VM] * 2,
        scratch_shapes=[
            vm((4, 8, 8, D)), vm((7, 7, D)), vm((24, 768)), vm((24, 768)), vm((256, D)), vm((96, D)), vm((96, D)), vm((96, D)), vm((96, D)),
            vm((2, 24, 384), F32), vm((2, 24, 384), F32),
            vm((1, 8, 4, 48, 384)), vm((1, 8, 4, 48, 384)),
            vm((2, 256, D)), vm((64, D), F32), vm((4, D), F32),
            vm((8, 768), F32), vm((8, 768), F32), vm((8, 768), F32), vm((8, 8, 768), F32),
            vm((8, 768), F32), vm((8, 768), F32), vm((8, 96, 192)), vm((8, 96, 192)),
            vm((2, 8, 4, 192, 256)), vm((2, 8, 4, 16, 128)), vm((2, 8, 4, 16, 384)), vm((2, 8, 4, 32, 256)),
            vm((1024, 512), F32), vm((1024, 512), F32), vm((256, D)), vm((8, 96, 256)), vm((96, 256)),
            dma((9,)), dma((5, 6, 7)), dma((5, 6, 7)), dma((5, 8)), dma((5, 8)), dma((32,)), dma((32,)),
        ],
        name="whole",
        compiler_params=pltpu.CompilerParams(collective_id=0, has_side_effects=True, vmem_limit_bytes=56 * 2**20),
    )(tile_feats, dw_weight, ln_gain, w_expand, w_contract, layer_scale, tile_owner.T, tissue_index, slide_embed, slide_gain,
      w_query.T, w_key.T, w_value.T, w_out, segment_level, dilate_rate, slide_length)


def solution(mesh):
    placed = (
        P("enc", None, None, None),
        P(),
        P(),
        P("enc", "mdl"),
        P("enc", "mdl"),
        P(),
        P("enc", None),
        P("enc", None),
        P("enc", None),
        P(),
        P(None, "mdl"),
        P(None, "mdl"),
        P(None, "mdl"),
        P("mdl", None),
        P("mdl"),
        P("mdl"),
        P(),
    )
    return jax.shard_map(
        body,
        mesh=mesh,
        in_specs=placed,
        out_specs=(P("enc", None), P("enc", "mdl")),
        check_vma=False,
    )
```

```python
import functools
import math

import jax
import jax.numpy as jnp
from jax import lax
from jax.experimental import pallas as pl
from jax.experimental.pallas import tpu as pltpu
from jax.sharding import PartitionSpec as P

MESH = pl.DeviceIdType.MESH
F32 = jnp.float32
BF16 = jnp.bfloat16
HD = 48
D = 1536
NEG = -1e30
NY, NX, NZ = 8, 4, 8


def wrap(v, n):
    return lax.rem(v + 2 * n, n)


def place():
    e = lax.axis_index("enc")
    m = lax.axis_index("mdl")
    return e, m, lax.rem(e, 2), lax.rem(e // 2, NX), e // (2 * NX)


def device(y, x, c, m):
    return (y * (2 * NX) + x * 2 + c, m)


class Gather:
    def __init__(self, wave, buf, sems, orders, direct, split=None, share=""):
        self.w, self.buf, self.orders, self.direct, self.split, self.share = wave, buf, orders, direct, split, share
        self.send, self.recv, self.dsend, self.drecv = sems
        self.e, self.m, self.c, self.x, self.y = place()

    def at(self, core, y, x):
        return self.buf.at[core if self.share else 0, y, x]

    def own(self):
        return (self.c if self.share else 0, self.y, self.x)

    def plan(self, core):
        first, second = self.orders[core]
        size = {"x": NX, "y": NY}
        n1, n2 = size[first], size[second]

        def go(axis, k):
            if axis == "x":
                return device(self.y, wrap(self.x + k, NX), core, self.m)
            return device(wrap(self.y + k, NY), self.x, core, self.m)

        p1, p2 = (self.x, self.y) if first == "x" else (self.y, self.x)

        def ref(i1, i2):
            return self.at(core, i2, i1) if first == "x" else self.at(core, i1, i2)

        steps = []
        if self.direct[core][0]:
            steps.append([(k - 1, ref(p1, p2), ref(wrap(p1 - k, n1), p2), go(first, k)) for k in range(1, n1)])
        else:
            for s in range(n1 // 2):
                step = []
                for d, sg in ((0, 1), (1, -1)):
                    p, q = ref(wrap(p1 - s * sg, n1), p2), ref(wrap(p1 - (s + 1) * sg, n1), p2)
                    if s == n1 // 2 - 1:
                        rows = self.buf.shape[3]
                        cut = pl.ds(0, self.split) if d == 0 else pl.ds(self.split, rows - self.split)
                        p, q = p.at[cut], q.at[cut]
                    step.append((d, p, q, go(first, sg)))
                steps.append(step)
        whole = pl.ds(0, n1)
        shared = {len(steps): [ref(whole, p2)]}
        if self.direct[core][1]:
            steps.append([(k - 1, ref(whole, p2), ref(whole, wrap(p2 - k, n2)), go(second, k)) for k in range(1, n2)])
        else:
            for s in range(n2 // 2):
                step = []
                last = s == n2 // 2 - 1
                for d, sg in ((0, 1), (1, -1)):
                    part = pl.ds(d * (n1 // 2), n1 // 2) if last else whole
                    step.append((d, ref(part, wrap(p2 - s * sg, n2)), ref(part, wrap(p2 - (s + 1) * sg, n2)), go(second, sg)))
                steps.append(step)
                far = [wrap(p2 + s + 1, n2)] if last else [wrap(p2 - s - 1, n2), wrap(p2 + s + 1, n2)]
                shared[len(steps)] = [ref(whole, k) for k in far]
        if self.share == "end":
            shared = {len(steps): [self.buf.at[core]]}
        return steps, (shared if self.share else {})

    def remote(self, ref, s, k, to):
        return pltpu.make_async_remote_copy(
            src_ref=ref, dst_ref=ref, send_sem=self.send.at[self.w, s, k], recv_sem=self.recv.at[self.w, s, k],
            device_id=to, device_id_type=MESH)

    def across(self, ref, k, core):
        return pltpu.make_async_remote_copy(
            src_ref=ref, dst_ref=ref, send_sem=self.dsend.at[self.w, k], recv_sem=self.drecv.at[self.w, k],
            device_id=device(self.y, self.x, 1 - core, self.m), device_id_type=MESH)

    def step(self, s):
        for core in (0, 1):
            steps, shared = self.plan(core)
            if s > len(steps):
                continue

            @pl.when(self.c == core)
            def _():
                if s > 0:
                    for k, _, q, to in steps[s - 1]:
                        self.remote(q, s - 1, k, to).wait_recv()
                if s < len(steps):
                    for k, p, _, to in steps[s]:
                        self.remote(p, s, k, to).start()
                k = 0
                for t, refs in shared.items():
                    for ref in refs:
                        if t == s:
                            self.across(ref, k, core).start()
                        k += 1

    def wait_shared(self, source):
        _, shared = self.plan(source)
        for k, ref in enumerate([r for refs in shared.values() for r in refs]):
            self.across(ref, k, 1 - source).wait_recv()

    def finish(self):
        for core in (0, 1):

            @pl.when(self.c == core)
            def _():
                self.wait_shared(1 - core)

    def drain(self):
        for core in (0, 1):
            steps, shared = self.plan(core)

            @pl.when(self.c == core)
            def _():
                for s, step in enumerate(steps):
                    for k, p, _, to in step:
                        self.remote(p, s, k, to).wait_send()
                for k, ref in enumerate([r for refs in shared.values() for r in refs]):
                    self.across(ref, k, core).wait_send()


def z_copies(src, dst, send, recv, first):
    e, m, _, _, _ = place()
    out = []
    for j in range(1, NZ):
        to, back = wrap(m + j, NZ), wrap(m - j, NZ)
        mk = lambda s, d: pltpu.make_async_remote_copy(
            src_ref=s, dst_ref=d, send_sem=send.at[first + j - 1], recv_sem=recv.at[first + j - 1],
            device_id=(e, to), device_id_type=MESH)
        out.append((mk(src(to), dst.at[m]), mk(src(to), dst.at[back])))
    return out


def normed_rows(values, gain, epsilon):
    center = values - jnp.mean(values, axis=-1, keepdims=True)
    spread = jnp.mean(center * center, axis=-1, keepdims=True)
    return center * lax.rsqrt(spread + epsilon) * gain


def whole(feats_h, dw_h, lng, we_h, wc_h, ls, owner_row, tissue, slide_h, sg, wq_h, wk_h, wv_h, wo_h, level, rate, length,
          emb, out,
          feats, dw, we, wc, slide, wq, wk, wv, wo,
          wxs, wxr, wb0, wb1, wc0, wc1, nb, conv, mf, dxs, dxr, zs, zb, zr, exs, exr, ws, wor,
          kvb, metab, fb, keyf, stored_query, s0, s1, four, pick_rows, ab, attn,
          lsem, send, recv, dsend, drecv, msend, mrecv):
    e, m, c, x, y = place()
    other = device(y, x, 1 - c, m)
    targets = [other]
    for sg_ in range(1, NX):
        targets.append(device(y, wrap(x + sg_, NX), c, m))
    for sg_ in range(1, NY):
        targets.append(device(wrap(y + sg_, NY), x, c, m))
    for j in range(1, NZ):
        targets.append((e, wrap(m + j, NZ)))
    barrier = pltpu.get_barrier_semaphore()
    for to in targets:
        pl.semaphore_signal(barrier, inc=1, device_id=to, device_id_type=MESH)

    loads = {}
    for i, (name, src, dst) in enumerate((("we", we_h, we), ("wc", wc_h, wc), ("slide", slide_h, slide), ("wk", wk_h, wk), ("wv", wv_h, wv),
                                          ("feats", feats_h, feats), ("dw", dw_h, dw), ("wo", wo_h, wo), ("wq", wq_h, wq))):
        loads[name] = pltpu.make_async_copy(src, dst, lsem.at[i])
        loads[name].start()
    sems = (send, recv, dsend, drecv)

    def across(src, dst, k):
        return pltpu.make_async_remote_copy(
            src_ref=src, dst_ref=dst, send_sem=msend.at[k], recv_sem=mrecv.at[k], device_id=other, device_id_type=MESH)

    nt = lambda a, b: lax.dot_general(a, b, (((1,), (1,)), ((), ())), preferred_element_type=F32)

    loads["we"].wait()
    loads["wc"].wait()
    for core in (0, 1):

        @pl.when(c == core)
        def _():
            lanes = pl.ds(384 * (1 - core), 384)
            wxs[0] = we[:, lanes].astype(F32)
            wxs[1] = wc[:, lanes].astype(F32)

    loads["slide"].wait()
    loads["wk"].wait()
    loads["wv"].wait()
    loads["wq"].wait()
    gain = sg[...].reshape(1, D)
    snorm = normed_rows(slide[...].astype(F32), gain, 1e-05).astype(BF16)
    for i, ref in enumerate((wk, wv)):
        kvb[c, y, x, pl.ds(96 * i, 96), :] = nt(ref[...], snorm).astype(BF16)
    c2 = HD ** -0.5 * math.log2(math.e)
    stored_query[...] = (nt(wq[...], snorm) * c2).astype(BF16)

    row = lax.broadcasted_iota(jnp.int32, (16, 128), 0)
    lane = lax.broadcasted_iota(jnp.int32, (16, 128), 1)
    info = jnp.where(row == 0, tissue[:, pl.ds(0, 128)].astype(F32), 0.0)
    info = jnp.where(row == 1, tissue[:, pl.ds(128, 128)].astype(F32), info)
    own = owner_row[...].astype(F32)
    for i in range(4):
        info = jnp.where((row - 2) * 128 + lane == 4 * e + i, own[:, i:i + 1], info)
    metab[c, y, x] = info.astype(BF16)

    pl.semaphore_wait(barrier, len(targets))
    cross_w = across(wxs, wxr, 0)
    cross_w.start()
    mixed = ("xy", "yx")
    g_w = [Gather(i, ref, sems, mixed, ((True, False), (False, False)), 16) for i, ref in enumerate((wb0, wb1, wc0, wc1))]
    g_kv = Gather(4, kvb, sems, mixed, ((True, False), (False, False)), 96, "step")
    g_meta = Gather(5, metab, sems, mixed, ((True, True), (True, True)), share="end")
    g_f = Gather(6, fb, sems, mixed, ((True, True), (True, True)), share="end")
    g_meta.step(0)
    cross_w.wait()
    for core in (0, 1):

        @pl.when(c == core)
        def _():
            lanes = pl.ds(384 * core, 384)
            for k, (src, dst) in enumerate(((we, (wb0, wb1)), (wc, (wc0, wc1)))):
                mine = src[:, lanes].astype(F32)
                pair = [mine, wxr[k]] if core == 0 else [wxr[k], mine]
                both = jnp.concatenate(pair, axis=0).astype(BF16)
                dst[0][0, y, x] = both[:, :128]
                dst[1][0, y, x] = both[:, 128:]

    for g in g_w:
        g.step(0)
    g_kv.step(0)

    loads["wo"].wait()
    for j in range(NZ):
        ws[j] = wo[:, 192 * j:192 * j + 192]
    wor[m] = ws[m]
    wo_copies = z_copies(lambda to: ws.at[to], wor, msend, mrecv, 16)
    for copy, _ in wo_copies:
        copy.start()

    loads["feats"].wait()
    loads["dw"].wait()
    sub = lax.broadcasted_iota(jnp.int32, (8, 8, 128), 1)

    def conv_tile(t):
        def chunk(k, carry):
            lanes = pl.ds(pl.multiple_of(k * 128, 128), 128)
            xs = feats[t, :, :, lanes].astype(F32)
            mf[pl.ds(t, 1), lanes] = jnp.sum(jnp.sum(xs, axis=0), axis=0, keepdims=True)
            weight = dw[:, :, lanes].astype(F32)
            total = [jnp.zeros((8, 128), F32)] * 8
            for col in range(7):
                off = col - 3
                if off == 0:
                    moved = xs
                else:
                    moved = pltpu.roll(xs, (-off) % 8, axis=1)
                    moved = jnp.where((sub + off >= 0) & (sub + off < 8), moved, 0.0)
                for r in range(7):
                    tap = weight[r, col:col + 1, :]
                    for h in range(8):
                        if 0 <= h + r - 3 < 8:
                            total[h] = total[h] + moved[h + r - 3] * tap
            for h in range(8):
                conv[pl.ds(8 * h, 8), lanes] = total[h]
            return carry

        lax.fori_loop(0, D // 128, chunk, 0)
        nb[c, pl.ds(64 * t, 64), :] = normed_rows(conv[...], lng[...].reshape(1, D), 1e-06).astype(BF16)

    def cross_n(t):
        ref = nb.at[c, pl.ds(64 * t, 64)]
        return across(ref, ref, 1 + t)

    after = {0: [(g, 1) for g in g_w] + [(g_meta, 1)], 1: [(g, 2) for g in g_w] + [(g_kv, 1)], 2: [(g, 3) for g in g_w] + [(g_meta, 2)],
             3: [(g, 4) for g in g_w] + [(g_kv, 2)] + [(g, t) for t in (5, 6) for g in g_w]}
    for t in range(4):
        conv_tile(t)
        cross_n(t).start()
        for g, s in after[t]:
            g.step(s)
    for t in range(4):
        cross_n(t).wait_send()
        ref = nb.at[1 - c, pl.ds(64 * t, 64)]
        across(ref, ref, 1 + t).wait_recv()

    sums = []
    for k in range(4):
        rows = nb[k // 2, pl.ds(128 * (k % 2), 128), :]
        pre = jnp.concatenate([jnp.dot(rows, ref[0].reshape(D, -1), preferred_element_type=F32) for ref in (wb0, wb1)], axis=1)
        act = (0.5 * pre * (1.0 + lax.erf(pre * (0.5 ** 0.5)))).astype(BF16).astype(F32)
        for i in range(2):
            sums.append(jnp.sum(act[64 * i:64 * i + 64], axis=0, keepdims=True))
    hsum = jnp.concatenate(sums, axis=0)
    high = hsum.astype(BF16)
    low = (hsum - high.astype(F32)).astype(BF16)
    part = 0.0
    for half in (high, low):
        part += nt(half[:, :128], wc0[0].reshape(D, 128)) + nt(half[:, 128:], wc1[0].reshape(D, 256))
    part = part * (ls[...].reshape(1, D) * (1.0 / 64.0))
    mine = mf[...] * (1.0 / 64.0)
    for core in (0, 1):

        @pl.when(c == core)
        def _():
            zs[...] = part[:, 768 * core:768 * core + 768]
            far = slice(768 * (1 - core), 768 * (1 - core) + 768)
            dxs[...] = jnp.concatenate([part[:, far], mine[:, far], jnp.zeros((4, 768), F32)], axis=0)

    cross_p = across(dxs, dxr, 5)
    cross_p.start()
    cross_p.wait()
    both = zs[...] + dxr[pl.ds(0, 8), :]
    zb[...] = jnp.concatenate([both[:, :384], both[:, 384:]], axis=0).astype(BF16)
    zr[m] = zb[...]
    four[...] = jnp.zeros((8, D), F32)
    zc = z_copies(lambda to: zb, zr, msend, mrecv, 8)
    for copy, _ in zc:
        copy.start()

    g_kv.step(3)
    g_meta.finish()
    info = [metab[k].reshape(32, 16, 128).astype(F32) for k in range(2)]
    owner = jnp.concatenate([sum(jnp.sum(i[:, 2 + k, :], axis=0, keepdims=True) for i in info) for k in range(2)], axis=1)
    strip_of = 2 * lax.broadcasted_iota(jnp.int32, (32, 256), 0)
    picks, spots = [], 0.0
    for k in range(2):
        rows = jnp.concatenate([info[k][:, 0, :], info[k][:, 1, :]], axis=1)
        pick = ((strip_of + k).astype(F32) == owner).astype(F32)
        picks.append(pick.astype(BF16))
        spots = spots + jnp.sum(pick * rows, axis=0, keepdims=True)
    row_id = lax.broadcasted_iota(jnp.int32, (256, 256), 0).astype(F32)
    at_row = row_id == spots
    at_row_bf = at_row.astype(F32).astype(BF16)
    gone = [nt(p, at_row_bf) for p in picks]

    hits = (at_row & (owner == e.astype(F32))).astype(F32).astype(BF16)
    covered = nt(jnp.ones((8, 256), BF16), hits)

    shard = lax.broadcasted_iota(jnp.int32, (1024, 256), 0)
    tile = lax.broadcasted_iota(jnp.int32, (1024, 256), 1)
    tile_row = (tile // 4 % 2) * 512 + tile // 8 * 16 + tile % 4
    for k in range(4):
        pick_rows[:, pl.ds(256 * k, 256)] = (shard == tile_row + 4 * k).astype(F32).astype(BF16)

    f = lax.broadcasted_iota(jnp.int32, (32, 256), 0)
    amount = jnp.where(f < 8, 10 + f % 4, jnp.where(f < 14, (f - 8) % 3, (f - 14) % 3))
    flipped = ((f >= 4) & (f < 8)) | ((f >= 11) & (f < 14)) | ((f >= 17) & (f < 20))
    rates = [rate[h].astype(F32) for h in range(2)]
    limit = length[0].astype(F32)

    def bits(pos):
        pos_f = pos.astype(F32)
        res = [(pos_f - r * jnp.floor((pos_f + 0.5) / r)).astype(jnp.int32) for r in rates]
        src = jnp.where(f < 8, pos, jnp.where(f < 14, res[0], res[1]))
        bit = (jnp.right_shift(src, amount) & 1).astype(F32)
        return jnp.where(f < 20, jnp.where(flipped, 1.0 - bit, bit), 0.0)

    def features(pos, dead):
        dead = jnp.where(pos.astype(F32) >= limit, 1.0, dead)
        return jnp.where(f == 20, dead, bits(pos)).astype(BF16)

    line = lax.broadcasted_iota(jnp.int32, (1, 256), 1)
    for k in range(64):
        core, chip = k // 32, k % 32
        keyf[core, chip // NX, chip % NX] = features(line + (2 * chip + core) * 256, gone[core][chip:chip + 1, :])

    qpos = line + e * 256
    qbits = 1.0 - bits(qpos)
    bias = []
    for h in range(2):
        live = (f < 8) & (f % 4 >= 4 - level[h])
        live = live | ((f >= 8 + 6 * h) & (f < 14 + 6 * h)) | (f == 20)
        bias.append(jnp.where(live, qbits * NEG, 0.0).astype(BF16))

    g_kv.step(4)
    for copy, back in zc:
        copy.wait_send()
        back.wait_recv()
    summed = jnp.sum(zr[...].astype(F32), axis=0)
    for core in (0, 1):

        @pl.when(c == core)
        def _():
            pair = [mine[:, 768 * core:768 * core + 768], dxr[pl.ds(8, 4), :]]
            exs[...] = jnp.concatenate([summed[:8], summed[8:]], axis=1) + jnp.concatenate(pair if core == 0 else pair[::-1], axis=0)

    cross_e = across(exs, exr, 6)
    cross_e.start()
    cross_e.wait()
    for core in (0, 1):

        @pl.when(c == core)
        def _():
            at = pl.ds(4 * core, 4)
            pair = [exs[at, :], exr[at, :]]
            four[pl.ds(0, 4), :] = jnp.concatenate(pair if core == 0 else pair[::-1], axis=1)

    mine4 = four[...].astype(BF16)
    emb[...] = mine4[:4]
    norm4 = normed_rows(mine4.astype(F32), gain, 1e-05).astype(BF16)
    k4, v4, q4 = nt(norm4, wk[...])[:4], nt(norm4, wv[...])[:4], (nt(norm4, wq[...]) * c2)[:4]
    for j in range(NZ):

        @pl.when(m == j)
        def _():
            cols = mine4.astype(F32)[:4, 192 * j:192 * j + 192]
            block = [jnp.concatenate([k4, cols[:, 128:160]], axis=1), jnp.concatenate([v4, cols[:, 160:192]], axis=1),
                     jnp.concatenate([q4, jnp.zeros((4, 32), F32)], axis=1), cols[:, :128]]
            fb[c, y, x] = jnp.concatenate(block, axis=0).astype(BF16)

    g_f.step(0)
    g_kv.step(5)
    g_f.step(1)
    g_f.step(2)
    g_f.finish()

    tn = lambda a, b: lax.dot_general(a, b, (((0,), (0,)), ((), ())), preferred_element_type=F32)
    every = tn(fb[...].reshape(1024, 128), pick_rows[...]).astype(BF16)
    fkey, fval = every[:96, :256], every[:96, 256:512]
    fresh_cols = jnp.concatenate([every[:, 768:], every[96:, :256], every[96:, 256:512]], axis=0)
    query = nt(every[:96, 512:768], hits)
    query = jnp.where(covered[:1] > 0.5, query, stored_query[...].astype(F32)).astype(BF16)
    ffeat = features((owner * 256.0 + spots).astype(jnp.int32), jnp.zeros((1, 256), F32))
    blank = jnp.zeros((HD, 256), BF16)
    qaug = jnp.concatenate([jnp.concatenate([query[:HD], blank, bias[0]], axis=0),
                            jnp.concatenate([blank, query[HD:], bias[1]], axis=0)], axis=1)
    def softened(s, state, values):
        top = state[0]
        new = jnp.maximum(top, jnp.max(s, axis=0, keepdims=True))
        p = jnp.exp2(s - new).astype(BF16)
        shrink = jnp.exp2(top - new)
        acc = [state[1 + h] * shrink[:, 256 * h:256 * h + 256]
               + jnp.dot(values[h], p[:, 256 * h:256 * h + 256], preferred_element_type=F32) for h in range(2)]
        return (new, *acc)

    def near(k):
        return (k + 1) // 2 * (1 - 2 * lax.rem(k, 2))

    def by_row(g, i):
        return 0, wrap(y + near(g), NY), i

    def by_column(g, i):
        return 1, 4 * lax.rem(g, 2) + i, wrap(x + near(g // 2), NX)

    def score(at, g, ref):
        places = [at(g, i) for i in range(4)]
        keys = jnp.concatenate(
            [jnp.concatenate([kvb[k, r, q, pl.ds(0, 96), :] for k, r, q in places], axis=1),
             jnp.concatenate([keyf[k, r, q] for k, r, q in places], axis=1)], axis=0)
        ref[...] = tn(keys, qaug)

    def soft(at, g, ref, state):
        places = [at(g, i) for i in range(4)]
        values = []
        for h in range(2):
            v = jnp.concatenate([kvb[k, r, q, pl.ds(96 + HD * h, HD), :] for k, r, q in places], axis=1)
            values.append(jnp.concatenate([v, jnp.ones((16, 1024), BF16)], axis=0))
        return softened(ref[...], state, values)

    def eight(at, state):
        score(at, 0, s0)

        def two(i, state):
            score(at, 2 * i + 1, s1)
            state = soft(at, 2 * i, s0, state)
            score(at, jnp.minimum(2 * i + 2, 7), s0)
            return soft(at, 2 * i + 1, s1, state)

        return lax.fori_loop(0, 4, two, state)

    state = (jnp.full((1, 512), NEG, F32), jnp.zeros((64, 256), F32), jnp.zeros((64, 256), F32))
    state = softened(tn(jnp.concatenate([fkey, ffeat], axis=0), qaug), state,
                     [jnp.concatenate([fval[HD * h:HD * h + HD], jnp.ones((16, 256), BF16)], axis=0) for h in range(2)])

    @pl.when(c == 1)
    def _():
        g_kv.wait_shared(0)

    state = eight(by_row, state)
    g_kv.step(6)

    @pl.when(c == 0)
    def _():
        g_kv.wait_shared(1)

    _, *acc = eight(by_column, state)
    for h in range(2):
        total = acc[h][HD:HD + 1]
        head = acc[h][:HD] / jnp.where(total > 0, total, 1.0)
        attn[pl.ds(HD * h, HD), :] = jnp.where(qpos.astype(F32) < limit, head, 0.0).astype(BF16)

    ab[m] = attn[...]
    copies = z_copies(lambda to: attn, ab, msend, mrecv, 24)
    for copy, _ in copies:
        copy.start()
    placed = nt(fresh_cols, hits)
    for j in range(NZ):

        @pl.when(m == j)
        def _():
            out[...] = jnp.where(covered[:1] > 0.5, placed, slide[:, 192 * j:192 * j + 192].astype(F32).T).astype(BF16)

    for copy, back in wo_copies:
        copy.wait_send()
        back.wait_recv()
    for g in (*g_w, g_kv, g_meta, g_f):
        g.drain()
    for copy, back in copies:
        copy.wait_send()
        back.wait_recv()
    total = tn(wor[...].reshape(768, 192), ab[...].reshape(768, 256))
    out[...] = (out[...].astype(F32) + total).astype(BF16)


VM = pl.BlockSpec(memory_space=pltpu.VMEM)
SM = pl.BlockSpec(memory_space=pltpu.SMEM)
ANY = pl.BlockSpec(memory_space=pl.ANY)


def shape(dims, dtype=BF16):
    return jax.ShapeDtypeStruct(dims, dtype)


def body(tile_feats, dw_weight, ln_gain, w_expand, w_contract, layer_scale, tile_owner, tissue_index, slide_embed,
         slide_gain, w_query, w_key, w_value, w_out, segment_level, dilate_rate, slide_length):
    dma = pltpu.SemaphoreType.DMA
    vm = lambda dims, dtype=BF16: pltpu.VMEM(dims, dtype)
    emb, out = pl.pallas_call(
        whole,
        out_shape=[shape((4, D)), shape((192, 256))],
        in_specs=[ANY, ANY, VM, ANY, ANY, VM, VM, VM, ANY, VM, ANY, ANY, ANY, ANY, SM, SM, SM],
        out_specs=[VM] * 2,
        scratch_shapes=[
            vm((4, 8, 8, D)), vm((7, 7, D)), vm((24, 768)), vm((24, 768)), vm((256, D)), vm((96, D)), vm((96, D)), vm((96, D)), vm((96, D)),
            vm((2, 24, 384), F32), vm((2, 24, 384), F32),
            vm((1, 8, 4, 48, 128)), vm((1, 8, 4, 48, 256)), vm((1, 8, 4, 48, 128)), vm((1, 8, 4, 48, 256)),
            vm((2, 256, D)), vm((64, D), F32), vm((4, D), F32),
            vm((16, 768), F32), vm((16, 768), F32), vm((8, 768), F32), vm((16, 384)), vm((8, 16, 384)),
            vm((8, 768), F32), vm((8, 768), F32), vm((8, 96, 192)), vm((8, 96, 192)),
            vm((2, 8, 4, 192, 256)), vm((2, 8, 4, 16, 128)), vm((2, 8, 4, 16, 128)), vm((2, 8, 4, 32, 256)), vm((96, 256)),
            vm((1024, 512), F32), vm((1024, 512), F32), vm((8, D), F32), vm((1024, 1024)), vm((8, 96, 256)), vm((96, 256)),
            dma((9,)), dma((7, 6, 7)), dma((7, 6, 7)), dma((7, 8)), dma((7, 8)), dma((32,)), dma((32,)),
        ],
        name="whole",
        compiler_params=pltpu.CompilerParams(collective_id=0, has_side_effects=True, vmem_limit_bytes=56 * 2**20),
    )(tile_feats, dw_weight, ln_gain, w_expand, w_contract, layer_scale, tile_owner.T, tissue_index, slide_embed, slide_gain,
      w_query.T, w_key.T, w_value.T, w_out, segment_level, dilate_rate, slide_length)
    return emb, out.T


def solution(mesh):
    placed = (
        P("enc", None, None, None),
        P(),
        P(),
        P("enc", "mdl"),
        P("enc", "mdl"),
        P(),
        P("enc", None),
        P("enc", None),
        P("enc", None),
        P(),
        P(None, "mdl"),
        P(None, "mdl"),
        P(None, "mdl"),
        P("mdl", None),
        P("mdl"),
        P("mdl"),
        P(),
    )
    return jax.shard_map(
        body,
        mesh=mesh,
        in_specs=placed,
        out_specs=(P("enc", None), P("enc", "mdl")),
        check_vma=False,
    )
```

```python
import functools
import math

import jax
import jax.numpy as jnp
from jax import lax
from jax.experimental import pallas as pl
from jax.experimental.pallas import tpu as pltpu
from jax.sharding import PartitionSpec as P

MESH = pl.DeviceIdType.MESH
F32 = jnp.float32
BF16 = jnp.bfloat16
HD = 48
D = 1536
NEG = -1e30
NY, NX, NZ = 8, 4, 8


def wrap(v, n):
    return lax.rem(v + 2 * n, n)


def place():
    e = lax.axis_index("enc")
    m = lax.axis_index("mdl")
    return e, m, lax.rem(e, 2), lax.rem(e // 2, NX), e // (2 * NX)


def device(y, x, c, m):
    return (y * (2 * NX) + x * 2 + c, m)


class Gather:
    def __init__(self, wave, buf, sems, orders, direct, split=None, share="", rows=None):
        self.w, self.buf, self.orders, self.direct, self.split, self.share = wave, buf, orders, direct, split, share
        self.rows = rows
        self.send, self.recv, self.dsend, self.drecv = sems
        self.e, self.m, self.c, self.x, self.y = place()

    def at(self, core, y, x):
        if self.rows is None:
            return self.buf.at[core if self.share else 0, y, x]
        return self.buf.at[core if self.share else 0, y, x, pl.ds(*self.rows)]

    def own(self):
        return (self.c if self.share else 0, self.y, self.x)

    def plan(self, core):
        first, second = self.orders[core]
        size = {"x": NX, "y": NY}
        n1, n2 = size[first], size[second]

        def go(axis, k):
            if axis == "x":
                return device(self.y, wrap(self.x + k, NX), core, self.m)
            return device(wrap(self.y + k, NY), self.x, core, self.m)

        p1, p2 = (self.x, self.y) if first == "x" else (self.y, self.x)

        def ref(i1, i2):
            return self.at(core, i2, i1) if first == "x" else self.at(core, i1, i2)

        steps = []
        if self.direct[core][0]:
            steps.append([(k - 1, ref(p1, p2), ref(wrap(p1 - k, n1), p2), go(first, k)) for k in range(1, n1)])
        else:
            for s in range(n1 // 2):
                step = []
                for d, sg in ((0, 1), (1, -1)):
                    p, q = ref(wrap(p1 - s * sg, n1), p2), ref(wrap(p1 - (s + 1) * sg, n1), p2)
                    if s == n1 // 2 - 1:
                        rows = self.rows[1] if self.rows else self.buf.shape[3]
                        cut = pl.ds(0, self.split) if d == 0 else pl.ds(self.split, rows - self.split)
                        p, q = p.at[cut], q.at[cut]
                    step.append((d, p, q, go(first, sg)))
                steps.append(step)
        whole = pl.ds(0, n1)
        shared = {len(steps): [ref(whole, p2)]}
        if self.direct[core][1]:
            steps.append([(k - 1, ref(whole, p2), ref(whole, wrap(p2 - k, n2)), go(second, k)) for k in range(1, n2)])
        else:
            for s in range(n2 // 2):
                step = []
                last = s == n2 // 2 - 1
                for d, sg in ((0, 1), (1, -1)):
                    part = pl.ds(d * (n1 // 2), n1 // 2) if last else whole
                    step.append((d, ref(part, wrap(p2 - s * sg, n2)), ref(part, wrap(p2 - (s + 1) * sg, n2)), go(second, sg)))
                steps.append(step)
                far = [wrap(p2 + s + 1, n2)] if last else [wrap(p2 - s - 1, n2), wrap(p2 + s + 1, n2)]
                shared[len(steps)] = [ref(whole, k) for k in far]
        if self.share == "end":
            shared = {len(steps): [self.buf.at[core]]}
        return steps, (shared if self.share else {})

    def remote(self, ref, s, k, to):
        return pltpu.make_async_remote_copy(
            src_ref=ref, dst_ref=ref, send_sem=self.send.at[self.w, s, k], recv_sem=self.recv.at[self.w, s, k],
            device_id=to, device_id_type=MESH)

    def across(self, ref, k, core):
        return pltpu.make_async_remote_copy(
            src_ref=ref, dst_ref=ref, send_sem=self.dsend.at[self.w, k], recv_sem=self.drecv.at[self.w, k],
            device_id=device(self.y, self.x, 1 - core, self.m), device_id_type=MESH)

    def step(self, s):
        for core in (0, 1):
            steps, shared = self.plan(core)
            if s > len(steps):
                continue

            @pl.when(self.c == core)
            def _():
                if s > 0:
                    for k, _, q, to in steps[s - 1]:
                        self.remote(q, s - 1, k, to).wait_recv()
                if s < len(steps):
                    for k, p, _, to in steps[s]:
                        self.remote(p, s, k, to).start()
                k = 0
                for t, refs in shared.items():
                    for ref in refs:
                        if t == s:
                            self.across(ref, k, core).start()
                        k += 1

    def wait_shared(self, source):
        _, shared = self.plan(source)
        for k, ref in enumerate([r for refs in shared.values() for r in refs]):
            self.across(ref, k, 1 - source).wait_recv()

    def finish(self):
        for core in (0, 1):

            @pl.when(self.c == core)
            def _():
                self.wait_shared(1 - core)

    def drain(self):
        for core in (0, 1):
            steps, shared = self.plan(core)

            @pl.when(self.c == core)
            def _():
                for s, step in enumerate(steps):
                    for k, p, _, to in step:
                        self.remote(p, s, k, to).wait_send()
                for k, ref in enumerate([r for refs in shared.values() for r in refs]):
                    self.across(ref, k, core).wait_send()


def z_copies(src, dst, send, recv, first):
    e, m, _, _, _ = place()
    out = []
    for j in range(1, NZ):
        to, back = wrap(m + j, NZ), wrap(m - j, NZ)
        mk = lambda s, d: pltpu.make_async_remote_copy(
            src_ref=s, dst_ref=d, send_sem=send.at[first + j - 1], recv_sem=recv.at[first + j - 1],
            device_id=(e, to), device_id_type=MESH)
        out.append((mk(src(to), dst.at[m]), mk(src(to), dst.at[back])))
    return out


def normed_rows(values, gain, epsilon):
    center = values - jnp.mean(values, axis=-1, keepdims=True)
    spread = jnp.mean(center * center, axis=-1, keepdims=True)
    return center * lax.rsqrt(spread + epsilon) * gain


def whole(feats_h, dw_h, lng, we_h, wc_h, ls, owner_row, tissue, slide_h, sg, wq_h, wk_h, wv_h, wo_h, level, rate, length,
          emb, out,
          feats, dw, we, wc, slide, wq, wk, wv, wo,
          wxs, wxr, wb0, wb1, wc0, wc1, nb, conv, mf, dxs, dxr, zs, zb, zr, exs, exr, ws, wor,
          kvb, metab, fb, keyf, stored_query, s0, s1, four, pick_rows, ab, attn,
          lsem, send, recv, dsend, drecv, msend, mrecv):
    e, m, c, x, y = place()
    other = device(y, x, 1 - c, m)
    targets = [other]
    for sg_ in range(1, NX):
        targets.append(device(y, wrap(x + sg_, NX), c, m))
    for sg_ in range(1, NY):
        targets.append(device(wrap(y + sg_, NY), x, c, m))
    for j in range(1, NZ):
        targets.append((e, wrap(m + j, NZ)))
    barrier = pltpu.get_barrier_semaphore()
    for to in targets:
        pl.semaphore_signal(barrier, inc=1, device_id=to, device_id_type=MESH)

    loads = {}
    for i, (name, src, dst) in enumerate((("we", we_h, we), ("wc", wc_h, wc), ("slide", slide_h, slide), ("wk", wk_h, wk), ("wv", wv_h, wv),
                                          ("feats", feats_h, feats), ("dw", dw_h, dw), ("wo", wo_h, wo), ("wq", wq_h, wq))):
        loads[name] = pltpu.make_async_copy(src, dst, lsem.at[i])
        loads[name].start()
    sems = (send, recv, dsend, drecv)

    def across(src, dst, k):
        return pltpu.make_async_remote_copy(
            src_ref=src, dst_ref=dst, send_sem=msend.at[k], recv_sem=mrecv.at[k], device_id=other, device_id_type=MESH)

    nt = lambda a, b: lax.dot_general(a, b, (((1,), (1,)), ((), ())), preferred_element_type=F32)

    loads["we"].wait()
    loads["wc"].wait()
    for core in (0, 1):

        @pl.when(c == core)
        def _():
            lanes = pl.ds(384 * (1 - core), 384)
            wxs[0] = we[:, lanes].astype(F32)
            wxs[1] = wc[:, lanes].astype(F32)

    loads["slide"].wait()
    loads["wk"].wait()
    loads["wv"].wait()
    loads["wq"].wait()
    gain = sg[...].reshape(1, D)
    snorm = normed_rows(slide[...].astype(F32), gain, 1e-05).astype(BF16)
    for i, ref in enumerate((wk, wv)):
        kvb[c, y, x, pl.ds(96 * i, 96), :] = nt(ref[...], snorm).astype(BF16)
    c2 = HD ** -0.5 * math.log2(math.e)
    stored_query[...] = (nt(wq[...], snorm) * c2).astype(BF16)

    row = lax.broadcasted_iota(jnp.int32, (16, 128), 0)
    lane = lax.broadcasted_iota(jnp.int32, (16, 128), 1)
    info = jnp.where(row == 0, tissue[:, pl.ds(0, 128)].astype(F32), 0.0)
    info = jnp.where(row == 1, tissue[:, pl.ds(128, 128)].astype(F32), info)
    own = owner_row[...].astype(F32)
    for i in range(4):
        info = jnp.where((row - 2) * 128 + lane == 4 * e + i, own[:, i:i + 1], info)
    metab[c, y, x] = info.astype(BF16)

    pl.semaphore_wait(barrier, len(targets))
    cross_w = across(wxs, wxr, 0)
    cross_w.start()
    mixed = ("xy", "yx")
    g_w = [Gather(i, ref, sems, mixed, ((True, False), (False, False)), 16) for i, ref in enumerate((wb0, wb1, wc0, wc1))]
    g_k, g_v = [Gather(4 + 3 * i, kvb, sems, mixed, ((True, False), (False, False)), 48, "step", (96 * i, 96)) for i in range(2)]
    g_meta = Gather(5, metab, sems, mixed, ((True, True), (True, True)), share="end")
    g_f = Gather(6, fb, sems, mixed, ((True, True), (True, True)), share="end")
    g_meta.step(0)
    cross_w.wait()
    for core in (0, 1):

        @pl.when(c == core)
        def _():
            lanes = pl.ds(384 * core, 384)
            for k, (src, dst) in enumerate(((we, (wb0, wb1)), (wc, (wc0, wc1)))):
                mine = src[:, lanes].astype(F32)
                pair = [mine, wxr[k]] if core == 0 else [wxr[k], mine]
                both = jnp.concatenate(pair, axis=0).astype(BF16)
                dst[0][0, y, x] = both[:, :128]
                dst[1][0, y, x] = both[:, 128:]

    for g in g_w:
        g.step(0)
    g_k.step(0)
    g_v.step(0)

    loads["wo"].wait()
    for j in range(NZ):
        ws[j] = wo[:, 192 * j:192 * j + 192]
    wor[m] = ws[m]
    wo_copies = z_copies(lambda to: ws.at[to], wor, msend, mrecv, 16)
    for copy, _ in wo_copies:
        copy.start()

    loads["feats"].wait()
    loads["dw"].wait()
    sub = lax.broadcasted_iota(jnp.int32, (8, 8, 128), 1)

    def conv_tile(t):
        def chunk(k, carry):
            lanes = pl.ds(pl.multiple_of(k * 128, 128), 128)
            xs = feats[t, :, :, lanes].astype(F32)
            mf[pl.ds(t, 1), lanes] = jnp.sum(jnp.sum(xs, axis=0), axis=0, keepdims=True)
            weight = dw[:, :, lanes].astype(F32)
            total = [jnp.zeros((8, 128), F32)] * 8
            for col in range(7):
                off = col - 3
                if off == 0:
                    moved = xs
                else:
                    moved = pltpu.roll(xs, (-off) % 8, axis=1)
                    moved = jnp.where((sub + off >= 0) & (sub + off < 8), moved, 0.0)
                for r in range(7):
                    tap = weight[r, col:col + 1, :]
                    for h in range(8):
                        if 0 <= h + r - 3 < 8:
                            total[h] = total[h] + moved[h + r - 3] * tap
            for h in range(8):
                conv[pl.ds(8 * h, 8), lanes] = total[h]
            return carry

        lax.fori_loop(0, D // 128, chunk, 0)
        nb[c, pl.ds(64 * t, 64), :] = normed_rows(conv[...], lng[...].reshape(1, D), 1e-06).astype(BF16)

    def cross_n(t):
        ref = nb.at[c, pl.ds(64 * t, 64)]
        return across(ref, ref, 1 + t)

    after = {0: [(g, 1) for g in g_w] + [(g_meta, 1)], 1: [(g, 2) for g in g_w] + [(g_k, 1), (g_v, 1)], 2: [(g, 3) for g in g_w] + [(g_meta, 2)],
             3: [(g, 4) for g in g_w] + [(g_k, 2), (g_v, 2)] + [(g, t) for t in (5, 6) for g in g_w]}
    for t in range(4):
        conv_tile(t)
        cross_n(t).start()
        for g, s in after[t]:
            g.step(s)
    for t in range(4):
        cross_n(t).wait_send()
        ref = nb.at[1 - c, pl.ds(64 * t, 64)]
        across(ref, ref, 1 + t).wait_recv()

    sums = []
    for k in range(4):
        rows = nb[k // 2, pl.ds(128 * (k % 2), 128), :]
        pre = jnp.concatenate([jnp.dot(rows, ref[0].reshape(D, -1), preferred_element_type=F32) for ref in (wb0, wb1)], axis=1)
        act = (0.5 * pre * (1.0 + lax.erf(pre * (0.5 ** 0.5)))).astype(BF16).astype(F32)
        for i in range(2):
            sums.append(jnp.sum(act[64 * i:64 * i + 64], axis=0, keepdims=True))
    hsum = jnp.concatenate(sums, axis=0)
    high = hsum.astype(BF16)
    low = (hsum - high.astype(F32)).astype(BF16)
    part = 0.0
    for half in (high, low):
        part += nt(half[:, :128], wc0[0].reshape(D, 128)) + nt(half[:, 128:], wc1[0].reshape(D, 256))
    part = part * (ls[...].reshape(1, D) * (1.0 / 64.0))
    mine = mf[...] * (1.0 / 64.0)
    for core in (0, 1):

        @pl.when(c == core)
        def _():
            zs[...] = part[:, 768 * core:768 * core + 768]
            far = slice(768 * (1 - core), 768 * (1 - core) + 768)
            dxs[...] = jnp.concatenate([part[:, far], mine[:, far], jnp.zeros((4, 768), F32)], axis=0)

    cross_p = across(dxs, dxr, 5)
    cross_p.start()
    cross_p.wait()
    both = zs[...] + dxr[pl.ds(0, 8), :]
    zb[...] = jnp.concatenate([both[:, :384], both[:, 384:]], axis=0).astype(BF16)
    zr[m] = zb[...]
    four[...] = jnp.zeros((8, D), F32)
    zc = z_copies(lambda to: zb, zr, msend, mrecv, 8)
    for copy, _ in zc:
        copy.start()

    g_k.step(3)
    g_v.step(3)
    g_meta.finish()
    info = [metab[k].reshape(32, 16, 128).astype(F32) for k in range(2)]
    owner = jnp.concatenate([sum(jnp.sum(i[:, 2 + k, :], axis=0, keepdims=True) for i in info) for k in range(2)], axis=1)
    strip_of = 2 * lax.broadcasted_iota(jnp.int32, (32, 256), 0)
    picks, spots = [], 0.0
    for k in range(2):
        rows = jnp.concatenate([info[k][:, 0, :], info[k][:, 1, :]], axis=1)
        pick = ((strip_of + k).astype(F32) == owner).astype(F32)
        picks.append(pick.astype(BF16))
        spots = spots + jnp.sum(pick * rows, axis=0, keepdims=True)
    row_id = lax.broadcasted_iota(jnp.int32, (256, 256), 0).astype(F32)
    at_row = row_id == spots
    at_row_bf = at_row.astype(F32).astype(BF16)
    gone = [nt(p, at_row_bf) for p in picks]

    hits = (at_row & (owner == e.astype(F32))).astype(F32).astype(BF16)
    covered = nt(jnp.ones((8, 256), BF16), hits)

    shard = lax.broadcasted_iota(jnp.int32, (1024, 256), 0)
    tile = lax.broadcasted_iota(jnp.int32, (1024, 256), 1)
    tile_row = (tile // 4 % 2) * 512 + tile // 8 * 16 + tile % 4
    for k in range(4):
        pick_rows[:, pl.ds(256 * k, 256)] = (shard == tile_row + 4 * k).astype(F32).astype(BF16)

    f = lax.broadcasted_iota(jnp.int32, (32, 256), 0)
    amount = jnp.where(f < 8, 10 + f % 4, jnp.where(f < 14, (f - 8) % 3, (f - 14) % 3))
    flipped = ((f >= 4) & (f < 8)) | ((f >= 11) & (f < 14)) | ((f >= 17) & (f < 20))
    rates = [rate[h].astype(F32) for h in range(2)]
    limit = length[0].astype(F32)

    def bits(pos):
        pos_f = pos.astype(F32)
        res = [(pos_f - r * jnp.floor((pos_f + 0.5) / r)).astype(jnp.int32) for r in rates]
        src = jnp.where(f < 8, pos, jnp.where(f < 14, res[0], res[1]))
        bit = (jnp.right_shift(src, amount) & 1).astype(F32)
        return jnp.where(f < 20, jnp.where(flipped, 1.0 - bit, bit), 0.0)

    def features(pos, dead):
        dead = jnp.where(pos.astype(F32) >= limit, 1.0, dead)
        return jnp.where(f == 20, dead, bits(pos)).astype(BF16)

    line = lax.broadcasted_iota(jnp.int32, (1, 256), 1)
    for k in range(64):
        core, chip = k // 32, k % 32
        keyf[core, chip // NX, chip % NX] = features(line + (2 * chip + core) * 256, gone[core][chip:chip + 1, :])

    qpos = line + e * 256
    qbits = 1.0 - bits(qpos)
    bias = []
    for h in range(2):
        live = (f < 8) & (f % 4 >= 4 - level[h])
        live = live | ((f >= 8 + 6 * h) & (f < 14 + 6 * h)) | (f == 20)
        bias.append(jnp.where(live, qbits * NEG, 0.0).astype(BF16))

    g_k.step(4)
    g_v.step(4)
    for copy, back in zc:
        copy.wait_send()
        back.wait_recv()
    summed = jnp.sum(zr[...].astype(F32), axis=0)
    for core in (0, 1):

        @pl.when(c == core)
        def _():
            pair = [mine[:, 768 * core:768 * core + 768], dxr[pl.ds(8, 4), :]]
            exs[...] = jnp.concatenate([summed[:8], summed[8:]], axis=1) + jnp.concatenate(pair if core == 0 else pair[::-1], axis=0)

    cross_e = across(exs, exr, 6)
    cross_e.start()
    cross_e.wait()
    for core in (0, 1):

        @pl.when(c == core)
        def _():
            at = pl.ds(4 * core, 4)
            pair = [exs[at, :], exr[at, :]]
            four[pl.ds(0, 4), :] = jnp.concatenate(pair if core == 0 else pair[::-1], axis=1)

    mine4 = four[...].astype(BF16)
    emb[...] = mine4[:4]
    norm4 = normed_rows(mine4.astype(F32), gain, 1e-05).astype(BF16)
    k4, v4, q4 = nt(norm4, wk[...])[:4], nt(norm4, wv[...])[:4], (nt(norm4, wq[...]) * c2)[:4]
    for j in range(NZ):

        @pl.when(m == j)
        def _():
            cols = mine4.astype(F32)[:4, 192 * j:192 * j + 192]
            block = [jnp.concatenate([k4, cols[:, 128:160]], axis=1), jnp.concatenate([v4, cols[:, 160:192]], axis=1),
                     jnp.concatenate([q4, jnp.zeros((4, 32), F32)], axis=1), cols[:, :128]]
            fb[c, y, x] = jnp.concatenate(block, axis=0).astype(BF16)

    g_f.step(0)
    g_f.step(1)
    g_k.step(5)
    g_v.step(5)
    g_f.step(2)
    g_f.finish()

    tn = lambda a, b: lax.dot_general(a, b, (((0,), (0,)), ((), ())), preferred_element_type=F32)
    every = tn(fb[...].reshape(1024, 128), pick_rows[...]).astype(BF16)
    fkey, fval = every[:96, :256], every[:96, 256:512]
    fresh_cols = jnp.concatenate([every[:, 768:], every[96:, :256], every[96:, 256:512]], axis=0)
    query = nt(every[:96, 512:768], hits)
    query = jnp.where(covered[:1] > 0.5, query, stored_query[...].astype(F32)).astype(BF16)
    ffeat = features((owner * 256.0 + spots).astype(jnp.int32), jnp.zeros((1, 256), F32))
    blank = jnp.zeros((HD, 256), BF16)
    qaug = jnp.concatenate([jnp.concatenate([query[:HD], blank, bias[0]], axis=0),
                            jnp.concatenate([blank, query[HD:], bias[1]], axis=0)], axis=1)
    def softened(s, state, values):
        top = state[0]
        new = jnp.maximum(top, jnp.max(s, axis=0, keepdims=True))
        p = jnp.exp2(s - new).astype(BF16)
        shrink = jnp.exp2(top - new)
        acc = [state[1 + h] * shrink[:, 256 * h:256 * h + 256]
               + jnp.dot(values[h], p[:, 256 * h:256 * h + 256], preferred_element_type=F32) for h in range(2)]
        return (new, *acc)

    def near(k):
        return (k + 1) // 2 * (1 - 2 * lax.rem(k, 2))

    def by_row(g, i):
        return 0, wrap(y + near(g), NY), i

    def by_column(g, i):
        return 1, 4 * lax.rem(g, 2) + i, wrap(x + near(g // 2), NX)

    def score(at, g, ref):
        places = [at(g, i) for i in range(4)]
        keys = jnp.concatenate(
            [jnp.concatenate([kvb[k, r, q, pl.ds(0, 96), :] for k, r, q in places], axis=1),
             jnp.concatenate([keyf[k, r, q] for k, r, q in places], axis=1)], axis=0)
        ref[...] = tn(keys, qaug)

    def soft(at, g, ref, state):
        places = [at(g, i) for i in range(4)]
        values = []
        for h in range(2):
            v = jnp.concatenate([kvb[k, r, q, pl.ds(96 + HD * h, HD), :] for k, r, q in places], axis=1)
            values.append(jnp.concatenate([v, jnp.ones((16, 1024), BF16)], axis=0))
        return softened(ref[...], state, values)

    def eight(at, state):
        score(at, 0, s0)

        def two(i, state):
            score(at, 2 * i + 1, s1)
            state = soft(at, 2 * i, s0, state)
            score(at, jnp.minimum(2 * i + 2, 7), s0)
            return soft(at, 2 * i + 1, s1, state)

        return lax.fori_loop(0, 4, two, state)

    state = (jnp.full((1, 512), NEG, F32), jnp.zeros((64, 256), F32), jnp.zeros((64, 256), F32))
    state = softened(tn(jnp.concatenate([fkey, ffeat], axis=0), qaug), state,
                     [jnp.concatenate([fval[HD * h:HD * h + HD], jnp.ones((16, 256), BF16)], axis=0) for h in range(2)])

    @pl.when(c == 1)
    def _():
        g_k.wait_shared(0)
        g_v.wait_shared(0)

    state = eight(by_row, state)
    g_k.step(6)
    g_v.step(6)

    @pl.when(c == 0)
    def _():
        g_k.wait_shared(1)
        g_v.wait_shared(1)

    _, *acc = eight(by_column, state)
    for h in range(2):
        total = acc[h][HD:HD + 1]
        head = acc[h][:HD] / jnp.where(total > 0, total, 1.0)
        attn[pl.ds(HD * h, HD), :] = jnp.where(qpos.astype(F32) < limit, head, 0.0).astype(BF16)

    ab[m] = attn[...]
    copies = z_copies(lambda to: attn, ab, msend, mrecv, 24)
    for copy, _ in copies:
        copy.start()
    placed = nt(fresh_cols, hits)
    for j in range(NZ):

        @pl.when(m == j)
        def _():
            out[...] = jnp.where(covered[:1] > 0.5, placed, slide[:, 192 * j:192 * j + 192].astype(F32).T).astype(BF16)

    for copy, back in wo_copies:
        copy.wait_send()
        back.wait_recv()
    for g in (*g_w, g_k, g_v, g_meta, g_f):
        g.drain()
    for copy, back in copies:
        copy.wait_send()
        back.wait_recv()
    total = tn(wor[...].reshape(768, 192), ab[...].reshape(768, 256))
    out[...] = (out[...].astype(F32) + total).astype(BF16)


VM = pl.BlockSpec(memory_space=pltpu.VMEM)
SM = pl.BlockSpec(memory_space=pltpu.SMEM)
ANY = pl.BlockSpec(memory_space=pl.ANY)


def shape(dims, dtype=BF16):
    return jax.ShapeDtypeStruct(dims, dtype)


def body(tile_feats, dw_weight, ln_gain, w_expand, w_contract, layer_scale, tile_owner, tissue_index, slide_embed,
         slide_gain, w_query, w_key, w_value, w_out, segment_level, dilate_rate, slide_length):
    dma = pltpu.SemaphoreType.DMA
    vm = lambda dims, dtype=BF16: pltpu.VMEM(dims, dtype)
    emb, out = pl.pallas_call(
        whole,
        out_shape=[shape((4, D)), shape((192, 256))],
        in_specs=[ANY, ANY, VM, ANY, ANY, VM, VM, VM, ANY, VM, ANY, ANY, ANY, ANY, SM, SM, SM],
        out_specs=[VM] * 2,
        scratch_shapes=[
            vm((4, 8, 8, D)), vm((7, 7, D)), vm((24, 768)), vm((24, 768)), vm((256, D)), vm((96, D)), vm((96, D)), vm((96, D)), vm((96, D)),
            vm((2, 24, 384), F32), vm((2, 24, 384), F32),
            vm((1, 8, 4, 48, 128)), vm((1, 8, 4, 48, 256)), vm((1, 8, 4, 48, 128)), vm((1, 8, 4, 48, 256)),
            vm((2, 256, D)), vm((64, D), F32), vm((4, D), F32),
            vm((16, 768), F32), vm((16, 768), F32), vm((8, 768), F32), vm((16, 384)), vm((8, 16, 384)),
            vm((8, 768), F32), vm((8, 768), F32), vm((8, 96, 192)), vm((8, 96, 192)),
            vm((2, 8, 4, 192, 256)), vm((2, 8, 4, 16, 128)), vm((2, 8, 4, 16, 128)), vm((2, 8, 4, 32, 256)), vm((96, 256)),
            vm((1024, 512), F32), vm((1024, 512), F32), vm((8, D), F32), vm((1024, 1024)), vm((8, 96, 256)), vm((96, 256)),
            dma((9,)), dma((8, 6, 7)), dma((8, 6, 7)), dma((8, 8)), dma((8, 8)), dma((32,)), dma((32,)),
        ],
        name="whole",
        compiler_params=pltpu.CompilerParams(collective_id=0, has_side_effects=True, vmem_limit_bytes=56 * 2**20),
    )(tile_feats, dw_weight, ln_gain, w_expand, w_contract, layer_scale, tile_owner.T, tissue_index, slide_embed, slide_gain,
      w_query.T, w_key.T, w_value.T, w_out, segment_level, dilate_rate, slide_length)
    return emb, out.T


def solution(mesh):
    placed = (
        P("enc", None, None, None),
        P(),
        P(),
        P("enc", "mdl"),
        P("enc", "mdl"),
        P(),
        P("enc", None),
        P("enc", None),
        P("enc", None),
        P(),
        P(None, "mdl"),
        P(None, "mdl"),
        P(None, "mdl"),
        P("mdl", None),
        P("mdl"),
        P("mdl"),
        P(),
    )
    return jax.shard_map(
        body,
        mesh=mesh,
        in_specs=placed,
        out_specs=(P("enc", None), P("enc", "mdl")),
        check_vma=False,
    )
```
